32 devices in a mesh: row: 8 (over z, y), col: 4 (over x, core).
Axes of the slice: x: 2, y: 2, z: 4, core: 2. Of those that a mesh axis runs over, the one named last changes fastest.
Arguments:
- features: bfloat16 [256, 128, 256], P('row', 'col'), may hold values from -6 to 6
- dw_kernel: bfloat16 [7, 7, 256], replicated, may hold values from -0.875 to 0.875
- dw_bias: float32 [256], replicated, may hold values from -4 to 4
- norm_gain: float32 [256], replicated, may hold values from 0.5 to 2
- norm_bias: float32 [256], replicated, may hold values from -3 to 3
- w_expand: bfloat16 [256, 1024], replicated, may hold values from -0.375 to 0.375
- b_expand: float32 [1024], replicated, may hold values from -3 to 3
- w_reduce: bfloat16 [1024, 256], replicated, may hold values from -0.1875 to 0.1875
- b_reduce: float32 [256], replicated, may hold values from -3 to 3
- layer_scale: float32 [256], replicated, may hold values from 0.5 to 2
- w_query: bfloat16 [256, 256], replicated, may hold values from -2 to 2
- w_keyval: bfloat16 [256, 512], replicated, may hold values from -0.375 to 0.375
- rel_bias: float32 [8, 7, 31], replicated, may hold values from -8 to 250, as said below
- w_out: bfloat16 [256, 256], replicated, may hold values from -0.75 to 0.75
Outputs:
- result: bfloat16 [256, 128, 256], P('row', 'col')
The draws below stay inside these ranges and needn't reach their ends.
Inputs may be any that keep to these rules, and one draw needn't show every extreme that they name: `rel_bias`: relative position bias of moderate size, with possibly a few much larger entries.
All inputs are finite; a program needn't handle non-finite values.
Results may differ from the reference program's by a relative error of at most 0.014.
Values may be sent and summed in bfloat16 or wider, within the bound.
A program may use at most 64 MiB of HBM per device.

```python
import math
import jax
import jax.numpy as jnp
from jax import lax

C = 256
FF = 1024
HEADS = 8
TILE = 32
HEIGHT = 256
WIDTH = 128
OFFSET_ROWS = 7
OFFSET_COLS = 31
N_ROW = 8


def draw_rel_bias(key, part):
    shape = (HEADS, OFFSET_ROWS, OFFSET_COLS)
    return jnp.clip(2.0 * jax.random.normal(key, shape, jnp.float32), -8.0, 8.0)


def levels(stream_key, shape, shards, low, top_value):
    def one(axis_at, shards_of):
        heights = jax.random.uniform(jax.random.fold_in(jax.random.fold_in(stream_key, 6), axis_at), (shards_of,), jnp.float32, low / len(shards), top_value / len(shards))
        return jnp.repeat(jnp.exp(heights), shape[axis_at] // shards_of).reshape((-1,) + (1,) * (len(shape) - axis_at - 1))

    level = one(*shards[0])
    for cut in shards[1:]:
        level = level * one(*cut)
    return level


def noise(stream_key, extent, width, most, split=(), held_as=jnp.bfloat16):
    result = jax.random.normal(stream_key, extent, jnp.float32) * width
    if len(split) > 0:
        result = levels(stream_key, extent, split, -0.22, 0.18) * result
    return jnp.clip(result, min=-most, max=most).astype(held_as)


def setup_inputs(seed: int = 0) -> dict:
    keys = jax.random.split(jax.random.key(seed), 15)
    features = noise(keys[0], (HEIGHT, WIDTH, C), 1.0, 6.0, ((0, 8), (1, 4)))
    dw_kernel = noise(keys[1], (7, 7, C), 49 ** -0.5, 0.875)
    dw_bias = noise(keys[2], (C,), 1.0, 4.0, (), jnp.float32)
    norm_gain = jnp.clip(jnp.exp(jax.random.uniform(keys[3], (C,), jnp.float32, math.log(0.5), math.log(2.0))), 0.5, 2.0)
    norm_bias = noise(keys[4], (C,), 0.5, 3.0, (), jnp.float32)
    w_expand = noise(keys[5], (C, FF), C ** -0.5, 0.375)
    b_expand = noise(keys[6], (FF,), 0.5, 3.0, (), jnp.float32)
    w_reduce = noise(keys[7], (FF, C), FF ** -0.5, 0.1875)
    b_reduce = noise(keys[8], (C,), 0.5, 3.0, (), jnp.float32)
    layer_scale = jnp.clip(jnp.exp(jax.random.uniform(keys[9], (C,), jnp.float32, math.log(0.5), math.log(2.0))), 0.5, 2.0)
    w_query = noise(keys[10], (C, C), (max(C // 32, 1)) ** -0.5, 2.0)
    w_keyval = noise(keys[11], (C, 2 * C), C ** -0.5, 0.375)
    rel_bias = draw_rel_bias(jax.random.fold_in(keys[14], 71), 0)
    w_out = noise(keys[13], (C, C), (C // 4) ** -0.5, 0.75)
    return dict(features=features, dw_kernel=dw_kernel, dw_bias=dw_bias, norm_gain=norm_gain, norm_bias=norm_bias, w_expand=w_expand, b_expand=b_expand, w_reduce=w_reduce, b_reduce=b_reduce, layer_scale=layer_scale, w_query=w_query, w_keyval=w_keyval, rel_bias=rel_bias, w_out=w_out)


def block_pass(padded, features, dw_kernel, dw_bias, norm_gain, norm_bias, w_expand, b_expand, w_reduce, b_reduce, layer_scale):
    tile_rows, tile_cols, channels = features.shape
    convolved = jnp.zeros((tile_rows, tile_cols, channels), jnp.float32)
    for tap_row in range(7):
        for tap_col in range(7):
            convolved = convolved + padded[tap_row:tap_row + tile_rows, tap_col:tap_col + tile_cols].astype(jnp.float32) * dw_kernel[tap_row, tap_col].astype(jnp.float32)
    convolved = convolved + dw_bias
    average = lax.optimization_barrier(jnp.mean(convolved, axis=-1, keepdims=True))
    centred = convolved - average
    variance = lax.optimization_barrier(jnp.mean(centred * centred, axis=-1, keepdims=True))
    normed = (centred * lax.rsqrt(variance + 1e-06) * norm_gain + norm_bias).astype(jnp.bfloat16).reshape(-1, channels)
    hidden = jax.nn.gelu(jnp.dot(normed, w_expand, preferred_element_type=jnp.float32) + b_expand, approximate=False).astype(jnp.bfloat16)
    reduced = jnp.dot(hidden, w_reduce, preferred_element_type=jnp.float32) + b_reduce
    summed = features.astype(jnp.float32).reshape(-1, channels) + layer_scale * reduced
    return summed.astype(jnp.bfloat16).reshape(tile_rows, tile_cols, channels)

def reference(features, dw_kernel, dw_bias, norm_gain, norm_bias, w_expand, b_expand, w_reduce, b_reduce, layer_scale, w_query, w_keyval, rel_bias, w_out):
    map_width = features.shape[1]
    channels = features.shape[2]
    region_rows = TILE // 8
    region_cols = map_width // 8
    token_count = region_rows * region_cols
    head_dim = channels // HEADS
    padded = jnp.pad(features, ((3, 3), (3, 3), (0, 0)))
    token_index = jnp.arange(token_count, dtype=jnp.int32)
    token_row = token_index // region_cols
    token_col = token_index % region_cols
    offset_rows = token_row[None, :] - token_row[:, None] + region_rows - 1
    offset_cols = token_col[None, :] - token_col[:, None] + region_cols - 1
    bias_full = rel_bias[:, offset_rows, offset_cols]

    def strip_pass(strip_index):
        band = lax.dynamic_slice_in_dim(padded, strip_index * TILE, TILE + 6, 0)
        centre = band[3:3 + TILE, 3:3 + map_width]
        block_out = block_pass(band, centre, dw_kernel, dw_bias, norm_gain, norm_bias, w_expand, b_expand, w_reduce, b_reduce, layer_scale)
        pooled = block_out.astype(jnp.float32).reshape(region_rows, 8, region_cols, 8, channels).mean(axis=(1, 3))
        pooled = pooled.astype(jnp.bfloat16).reshape(token_count, channels)
        queries = jnp.dot(pooled, w_query, preferred_element_type=jnp.float32).astype(jnp.bfloat16)
        keyval = jnp.dot(pooled, w_keyval, preferred_element_type=jnp.float32).astype(jnp.bfloat16)
        query_heads = queries.astype(jnp.float32).reshape(token_count, HEADS, head_dim)
        key_heads = keyval[:, :channels].astype(jnp.float32).reshape(token_count, HEADS, head_dim)
        value_heads = keyval[:, channels:].astype(jnp.float32).reshape(token_count, HEADS, head_dim)
        scores = jnp.einsum('qhd,khd->hqk', query_heads, key_heads) / jnp.sqrt(jnp.float32(head_dim)) + bias_full
        attn = jax.nn.softmax(scores, axis=-1).astype(jnp.bfloat16)
        context = jnp.einsum('hqk,khd->qhd', attn.astype(jnp.float32), value_heads).reshape(token_count, channels).astype(jnp.bfloat16)
        lifted = jnp.dot(context, w_out, preferred_element_type=jnp.float32).reshape(region_rows, 1, region_cols, 1, channels)
        spread = jnp.broadcast_to(lifted, (region_rows, 8, region_cols, 8, channels)).reshape(TILE, map_width, channels)
        return (block_out.astype(jnp.float32) + spread).astype(jnp.bfloat16)
    bands = lax.map(strip_pass, jnp.arange(N_ROW, dtype=jnp.int32))
    return bands.reshape(N_ROW * TILE, map_width, channels)
```

```python
import functools

import jax
import jax.numpy as jnp
from jax import lax
from jax.experimental import pallas as pl
from jax.experimental.pallas import tpu as pltpu
from jax.sharding import PartitionSpec as P

HEADS = 8
T = 32
W = 48
L = 8
MESH = pl.DeviceIdType.MESH
F32 = jnp.float32
BF16 = jnp.bfloat16


def dot(a, b):
    return jnp.dot(a, b, preferred_element_type=F32)


def gelu(x):
    return (0.5 * x) * (1.0 + lax.erf(x * 0.7071067811865476))


def kernel(
    n_row,
    n_col,
    feat,
    dw,
    dw_bias,
    gain,
    nbias,
    we_hbm,
    b_exp,
    wr_hbm,
    b_red,
    scale,
    wq_hbm,
    wkv_hbm,
    table,
    wo_hbm,
    out,
    we,
    wr,
    wq,
    wkv,
    wo,
    xs,
    taps,
    wb,
    norm,
    block,
    psum,
    bias,
    stage,
    rowbuf,
    colbuf,
    corner,
    gath,
    wsem,
    send_sem,
    recv_sem,
    gsend,
    grecv,
):
    row = lax.axis_index("row")
    col = lax.axis_index("col")
    span = 4 * n_col
    stride = 2 * span
    keys = 4 * stride

    weights = [
        pltpu.make_async_copy(s, d, wsem.at[k])
        for k, (s, d) in enumerate(
            ((we_hbm, we), (wr_hbm, wr), (wq_hbm, wq), (wkv_hbm, wkv), (wo_hbm, wo))
        )
    ]
    for c in weights:
        c.start()

    up, down = row > 0, row < n_row - 1
    left, right = col > 0, col < n_col - 1
    both = jnp.logical_and
    near = (
        (up, -1, 0),
        (down, 1, 0),
        (left, 0, -1),
        (right, 0, 1),
        (both(up, left), -1, -1),
        (both(up, right), -1, 1),
        (both(down, left), 1, -1),
        (both(down, right), 1, 1),
    )
    barrier = pltpu.get_barrier_semaphore()
    for cond, dr, dc in near:
        if dr != 0:

            @pl.when(cond)
            def _(dr=dr, dc=dc):
                pl.semaphore_signal(
                    barrier, inc=1, device_id=(row + dr, col + dc), device_id_type=MESH
                )

    for d in range(1, n_col):
        pl.semaphore_signal(
            barrier, inc=1, device_id=(row, lax.rem(col + d, n_col)), device_id_type=MESH
        )

    for h in range(2):
        lanes = slice(h * 128, h * 128 + 128)
        xs[h, 0 : 3 * W] = jnp.zeros((3 * W, 128), F32)
        xs[h, 35 * W : 38 * W] = jnp.zeros((3 * W, 128), F32)

    def widen(r, carry):
        base = pl.multiple_of((r + 3) * W, 16)
        v = feat[r].astype(F32)
        zero = jnp.zeros((8, 128), F32)
        for h in range(2):
            xs[h, pl.ds(base, 8)] = zero
            xs[h, pl.ds(base + L, T)] = v[:, h * 128 : h * 128 + 128]
            xs[h, pl.ds(base + L + T, 8)] = zero
        return carry

    lax.fori_loop(0, T, widen, 0)
    for side, first in ((0, 0), (1, T - 3)):
        for c in range(3):
            for h in range(2):
                stage[side, c, :, h * 128 : h * 128 + 128] = xs[
                    h, pl.ds(3 * W + L + first + c, T, stride=W)
                ].astype(BF16)

    number = lambda c: c.astype(jnp.int32)
    across = 1 + number(left) + number(right)
    pl.semaphore_wait(barrier, n_col - 1 + across * (number(up) + number(down)))

    def remote(src, dst, k, dr, dc):
        return pltpu.make_async_remote_copy(
            src_ref=src,
            dst_ref=dst,
            send_sem=send_sem.at[k],
            recv_sem=recv_sem.at[k],
            device_id=(row + dr, col + dc),
            device_id_type=MESH,
        )

    plan = (
        (feat.at[0:3], rowbuf.at[1]),
        (feat.at[T - 3 : T], rowbuf.at[0]),
        (stage.at[0], colbuf.at[1]),
        (stage.at[1], colbuf.at[0]),
        (stage.at[0, :, 0:16], corner.at[3]),
        (stage.at[1, :, 0:16], corner.at[2]),
        (stage.at[0, :, 16:32], corner.at[1]),
        (stage.at[1, :, 16:32], corner.at[0]),
    )
    opposite = (1, 0, 3, 2, 7, 6, 5, 4)
    sends = [remote(s, d, k, near[k][1], near[k][2]) for k, (s, d) in enumerate(plan)]
    for k, c in enumerate(sends):

        @pl.when(near[k][0])
        def _(c=c):
            c.start()

    for a in range(7):
        v = dw[a].astype(F32)
        for b in range(7):
            for h in range(2):
                wb[h, a * 7 + b] = jnp.broadcast_to(
                    v[b : b + 1, h * 128 : h * 128 + 128], (8, 128)
                )
    lane = lax.broadcasted_iota(jnp.int32, (8, keys), 1)
    valid = lax.rem(lane, stride) < span
    for r in range(4):
        t = table[r]
        for c in range(4):
            shift = keys - (span - 1) + 4 * col + c
            moved = pltpu.roll(t, shift, 1)
            bias[r * 4 + c] = jnp.where(valid, moved, -1e30)

    def halo(k):
        return sends[opposite[k]].wait_recv

    for k in range(2):

        @pl.when(near[k][0])
        def _(k=k):
            halo(k)()
            for q in range(3):
                v = rowbuf[k, q].astype(F32)
                r = q if k == 0 else T + 3 + q
                for h in range(2):
                    xs[h, r * W + L : r * W + L + T] = v[:, h * 128 : h * 128 + 128]

    for k in range(2):

        @pl.when(near[2 + k][0])
        def _(k=k):
            halo(2 + k)()
            for c in range(3):
                v = colbuf[k, c].astype(F32)
                first = 3 * W + (L - 3 if k == 0 else L + T) + c
                for h in range(2):
                    xs[h, pl.ds(first, T, stride=W)] = v[:, h * 128 : h * 128 + 128]

    for k in range(4):

        @pl.when(near[4 + k][0])
        def _(k=k):
            halo(4 + k)()
            low, far = k >= 2, k % 2 == 1
            for c in range(3):
                v = corner[k, c].astype(F32)
                for q in range(3):
                    at = (T + 3 + q if low else q) * W + (L + T if far else L - 3) + c
                    s = q if low else 13 + q
                    for h in range(2):
                        xs[h, at : at + 1] = v[s : s + 1, h * 128 : h * 128 + 128]

    def spread_rows(r, carry):
        for h in range(2):
            for m in range(10):
                taps[h, m, r] = xs[h, pl.ds(r * W + (L - 3) + m, 8, stride=4)]
        return carry

    lax.fori_loop(0, T + 6, spread_rows, 0)

    weights[0].wait()
    weights[1].wait()

    def region_row(i, carry):
        def column(j, carry):
            x = []
            for h in range(2):
                acc = jnp.broadcast_to(
                    dw_bias[:, h * 128 : h * 128 + 128].reshape(1, 1, 128), (8, 8, 128)
                )
                for b in range(7):
                    slab = taps[h, j + b, pl.ds(i * 8, 14)]
                    for a in range(7):
                        acc = acc + slab[a : a + 8] * wb[h, a * 7 + b]
                x.append(acc.reshape(64, 128))
            mean = (
                jnp.sum(x[0] + x[1], axis=-1, keepdims=True) * (1.0 / 256.0)
            )
            x = [v - mean for v in x]
            var = jnp.sum(x[0] * x[0] + x[1] * x[1], axis=-1, keepdims=True) * (1.0 / 256.0)
            inv = lax.rsqrt(var + 1e-06)
            for h in range(2):
                lanes = slice(h * 128, h * 128 + 128)
                norm[pl.ds(pl.multiple_of(j * 64, 64), 64), lanes] = (
                    x[h] * inv * gain[:, lanes] + nbias[:, lanes]
                ).astype(BF16)
            return carry

        lax.fori_loop(0, 4, column, 0)
        n = norm[...]
        red = jnp.zeros((256, 256), F32)
        for f in range(4):
            part = slice(f * 256, f * 256 + 256)
            hid = gelu(dot(n, we[:, part]) + b_exp[:, part]).astype(BF16)
            red = red + dot(hid, wr[part, :])
        red = scale[...] * (red + b_red[...])
        for h in range(2):
            total = jnp.zeros((8, 128), F32)
            for j in range(4):
                v = red[j * 64 : j * 64 + 64, h * 128 : h * 128 + 128].reshape(8, 8, 128)
                v = (v + taps[h, j + 3, pl.ds(i * 8 + 3, 8)]).astype(BF16).astype(F32)
                total = total + jnp.sum(v, axis=0)
                for r in range(8):
                    block[h, pl.ds((i * 8 + r) * T + j, 8, stride=4)] = v[r]
            psum[h, pl.ds(pl.multiple_of(i * 8, 8), 8)] = total
        return carry

    lax.fori_loop(0, 4, region_row, 0)

    pooled = jnp.concatenate(
        [
            (psum[h, pl.ds(0, 16, stride=2)] + psum[h, pl.ds(1, 16, stride=2)]) * (1.0 / 64.0)
            for h in range(2)
        ],
        axis=1,
    ).astype(BF16)
    gath[col] = pooled
    gathers = []
    for d in range(1, n_col):
        c = pltpu.make_async_remote_copy(
            src_ref=gath.at[col],
            dst_ref=gath.at[col],
            send_sem=gsend.at[d - 1],
            recv_sem=grecv.at[d - 1],
            device_id=(row, lax.rem(col + d, n_col)),
            device_id_type=MESH,
        )
        c.start()
        gathers.append(c)
    weights[2].wait()
    weights[3].wait()
    weights[4].wait()
    queries = dot(pooled, wq[...]).astype(BF16).astype(F32)
    channel = lax.broadcasted_iota(jnp.int32, (8, 256), 1)
    head = lax.broadcasted_iota(jnp.int32, (8, 256), 0)
    own = ((channel >= head * 32) & (channel < head * 32 + 32)).astype(F32)
    spread = (queries[:, None, :] * own[None]).reshape(128, 256).astype(BF16)
    key = lax.broadcasted_iota(jnp.int32, (keys, 16 * n_col), 0)
    token = lax.broadcasted_iota(jnp.int32, (keys, 16 * n_col), 1)
    place = ((token % 16) // 4) * stride + (token // 16) * 4 + token % 4
    pick = (key == place).astype(F32).astype(BF16)
    for k, c in enumerate(sends):

        @pl.when(near[k][0])
        def _(c=c):
            c.wait_send()

    for c in gathers:
        c.wait()
    tokens = gath[...].reshape(16 * n_col, 256)
    ordered = dot(pick, tokens).astype(BF16)
    keyval = dot(ordered, wkv[...]).astype(BF16)
    scores = lax.dot_general(
        spread, keyval[:, :256], (((1,), (1,)), ((), ())), preferred_element_type=F32
    )
    scores = scores * (1.0 / 32.0**0.5) + bias[...].reshape(128, keys)
    top = jnp.max(scores, axis=-1, keepdims=True)
    e = jnp.exp(scores - top)
    attn = (e / jnp.sum(e, axis=-1, keepdims=True)).astype(BF16)
    ctx = dot(attn, keyval[:, 256:]).reshape(16, 8, 256)
    ctx = jnp.sum(ctx * own[None], axis=1).astype(BF16)
    psum_lift = dot(ctx, wo[...])
    for g in range(16):
        norm_row = psum_lift[g : g + 1]
        wb[0, g] = jnp.broadcast_to(norm_row[:, :128], (8, 128))
        wb[1, g] = jnp.broadcast_to(norm_row[:, 128:], (8, 128))

    def finish(r, carry):
        i = r // 8
        parts = []
        for h in range(2):
            v = block[h, pl.ds(pl.multiple_of(r * T, T), T)].reshape(4, 8, 128)
            parts.append((v + wb[h, pl.ds(i * 4, 4)]).reshape(T, 128))
        out[r] = jnp.concatenate(parts, axis=1).astype(BF16)
        return carry

    lax.fori_loop(0, T, finish, 0)


def shards(
    n_row,
    n_col,
    features,
    dw_kernel,
    dw_bias,
    norm_gain,
    norm_bias,
    w_expand,
    b_expand,
    w_reduce,
    b_reduce,
    layer_scale,
    w_query,
    w_keyval,
    rel_bias,
    w_out,
):
    stride = 8 * n_col
    keys = 4 * stride
    padded = jnp.pad(rel_bias, ((0, 0), (0, 0), (0, 1)))
    table = jnp.stack([padded[:, 3 - r : 7 - r].reshape(HEADS, keys) for r in range(4)])
    vmem = pl.BlockSpec(memory_space=pltpu.VMEM)
    hbm = pl.BlockSpec(memory_space=pl.ANY)
    lane = lambda v: v.reshape(1, -1)
    return pl.pallas_call(
        functools.partial(kernel, n_row, n_col),
        out_shape=jax.ShapeDtypeStruct(features.shape, BF16),
        in_specs=[vmem] * 5 + [hbm, vmem, hbm, vmem, vmem, hbm, hbm, vmem, hbm],
        out_specs=vmem,
        scratch_shapes=[
            pltpu.VMEM(w_expand.shape, BF16),
            pltpu.VMEM(w_reduce.shape, BF16),
            pltpu.VMEM(w_query.shape, BF16),
            pltpu.VMEM(w_keyval.shape, BF16),
            pltpu.VMEM(w_out.shape, BF16),
            pltpu.VMEM((2, (T + 6) * W, 128), F32),
            pltpu.VMEM((2, 10, T + 6, 8, 128), F32),
            pltpu.VMEM((2, 49, 8, 128), F32),
            pltpu.VMEM((256, 256), BF16),
            pltpu.VMEM((2, T * T, 128), F32),
            pltpu.VMEM((2, 32, 128), F32),
            pltpu.VMEM((16, 8, keys), F32),
            pltpu.VMEM((2, 3, T, 256), BF16),
            pltpu.VMEM((2, 3, T, 256), BF16),
            pltpu.VMEM((2, 3, T, 256), BF16),
            pltpu.VMEM((4, 3, 16, 256), BF16),
            pltpu.VMEM((n_col, 16, 256), BF16),
            pltpu.SemaphoreType.DMA((5,)),
            pltpu.SemaphoreType.DMA((8,)),
            pltpu.SemaphoreType.DMA((8,)),
            pltpu.SemaphoreType.DMA((n_col - 1,)),
            pltpu.SemaphoreType.DMA((n_col - 1,)),
        ],
        compiler_params=pltpu.CompilerParams(
            collective_id=0, has_side_effects=True, vmem_limit_bytes=40 * 1024 * 1024
        ),
    )(
        features,
        dw_kernel,
        lane(dw_bias),
        lane(norm_gain),
        lane(norm_bias),
        w_expand,
        lane(b_expand),
        w_reduce,
        lane(b_reduce),
        lane(layer_scale),
        w_query,
        w_keyval,
        table,
        w_out,
    )


def solution(mesh):
    return jax.shard_map(
        functools.partial(shards, mesh.shape["row"], mesh.shape["col"]),
        mesh=mesh,
        in_specs=(P("row", "col", None),) + (P(),) * 13,
        out_specs=P("row", "col", None),
        check_vma=False,
    )
```

```python
import functools

import jax
import jax.numpy as jnp
from jax import lax
from jax.experimental import pallas as pl
from jax.experimental.pallas import tpu as pltpu
from jax.sharding import PartitionSpec as P

HEADS = 8
T = 32
W = 48
L = 8
MESH = pl.DeviceIdType.MESH
F32 = jnp.float32
BF16 = jnp.bfloat16


def dot(a, b):
    return jnp.dot(a, b, preferred_element_type=F32)


def gelu(x):
    size = jnp.abs(x)
    q = 1.0 + (0.3275911 * 0.7071067811865476) * size
    t = pl.reciprocal(q, approx=True)
    t = t * (2.0 - q * t)
    p = 0.5 * 1.061405429 * t - 0.5 * 1.453152027
    p = p * t + 0.5 * 1.421413741
    p = p * t - 0.5 * 0.284496736
    p = p * t + 0.5 * 0.254829592
    tail = (p * t) * jnp.exp2((x * x) * (-0.5 * 1.4426950408889634))
    return jnp.maximum(x, 0.0) - size * tail


def kernel(
    n_row,
    n_col,
    *refs,
):
    sources, out, local, rest = refs[:14], refs[14], refs[15:29], refs[29:]
    body(n_row, n_col, sources, out, local, *local, *rest)


def body(
    n_row,
    n_col,
    sources,
    out,
    local,
    feat,
    dw,
    dw_bias,
    gain,
    nbias,
    we,
    b_exp,
    wr,
    b_red,
    scale,
    wq,
    wkv,
    rel,
    wo,
    table,
    xs,
    taps,
    wb,
    conv,
    norm,
    block,
    psum,
    bias,
    stage,
    rowbuf,
    colbuf,
    corner,
    gath,
    wsem,
    send_sem,
    recv_sem,
    gsend,
    grecv,
):
    row = lax.axis_index("row")
    col = lax.axis_index("col")
    span = 4 * n_col
    stride = 2 * span
    keys = 4 * stride

    loads = [
        pltpu.make_async_copy(sources[k], local[k], wsem.at[k]) for k in range(len(local))
    ]
    for c in loads:
        c.start()

    up, down = row > 0, row < n_row - 1
    left, right = col > 0, col < n_col - 1
    both = jnp.logical_and
    near = (
        (up, -1, 0),
        (down, 1, 0),
        (left, 0, -1),
        (right, 0, 1),
        (both(up, left), -1, -1),
        (both(up, right), -1, 1),
        (both(down, left), 1, -1),
        (both(down, right), 1, 1),
    )
    barrier = pltpu.get_barrier_semaphore()
    for cond, dr, dc in near:
        if dr != 0:

            @pl.when(cond)
            def _(dr=dr, dc=dc):
                pl.semaphore_signal(
                    barrier, inc=1, device_id=(row + dr, col + dc), device_id_type=MESH
                )

    for d in range(1, n_col):
        pl.semaphore_signal(
            barrier, inc=1, device_id=(row, lax.rem(col + d, n_col)), device_id_type=MESH
        )

    for h in range(2):
        lanes = slice(h * 128, h * 128 + 128)
        xs[h, 0 : 3 * W] = jnp.zeros((3 * W, 128), F32)
        xs[h, 35 * W : 38 * W] = jnp.zeros((3 * W, 128), F32)

    def widen(r, carry):
        base = pl.multiple_of((r + 3) * W, 16)
        v = feat[r].astype(F32)
        zero = jnp.zeros((8, 128), F32)
        for h in range(2):
            xs[h, pl.ds(base, 8)] = zero
            xs[h, pl.ds(base + L, T)] = v[:, h * 128 : h * 128 + 128]
            xs[h, pl.ds(base + L + T, 8)] = zero
        return carry

    loads[0].wait()
    lax.fori_loop(0, T, widen, 0)
    for side, first in ((0, 0), (1, T - 3)):
        for c in range(3):
            for h in range(2):
                stage[side, c, :, h * 128 : h * 128 + 128] = xs[
                    h, pl.ds(3 * W + L + first + c, T, stride=W)
                ].astype(BF16)

    number = lambda c: c.astype(jnp.int32)
    across = 1 + number(left) + number(right)
    pl.semaphore_wait(barrier, n_col - 1 + across * (number(up) + number(down)))

    def remote(src, dst, k, dr, dc):
        return pltpu.make_async_remote_copy(
            src_ref=src,
            dst_ref=dst,
            send_sem=send_sem.at[k],
            recv_sem=recv_sem.at[k],
            device_id=(row + dr, col + dc),
            device_id_type=MESH,
        )

    plan = (
        (feat.at[0:3], rowbuf.at[1]),
        (feat.at[T - 3 : T], rowbuf.at[0]),
        (stage.at[0], colbuf.at[1]),
        (stage.at[1], colbuf.at[0]),
        (stage.at[0, :, 0:16], corner.at[3]),
        (stage.at[1, :, 0:16], corner.at[2]),
        (stage.at[0, :, 16:32], corner.at[1]),
        (stage.at[1, :, 16:32], corner.at[0]),
    )
    opposite = (1, 0, 3, 2, 7, 6, 5, 4)
    sends = [remote(s, d, k, near[k][1], near[k][2]) for k, (s, d) in enumerate(plan)]
    for k, c in enumerate(sends):

        @pl.when(near[k][0])
        def _(c=c):
            c.start()

    for k in (1, 2, 3, 4, 6, 8, 9, 12):
        loads[k].wait()
    for a in range(7):
        v = dw[a].astype(F32)
        for b in range(7):
            for h in range(2):
                wb[h, a * 7 + b] = jnp.broadcast_to(
                    v[b : b + 1, h * 128 : h * 128 + 128], (8, 128)
                )
    lane = lax.broadcasted_iota(jnp.int32, (8, keys), 1)
    valid = lax.rem(lane, stride) < span
    table[...] = jnp.zeros(table.shape, F32)
    for r in range(4):
        for k in range(4):
            width = 2 * span - 1
            table[r, :, k * stride : k * stride + width] = rel[k - r + 3]
        t = table[r]
        for c in range(4):
            shift = keys - (span - 1) + 4 * col + c
            moved = pltpu.roll(t, shift, 1)
            bias[r * 4 + c] = jnp.where(valid, moved, -1e30)

    def halo(k):
        return sends[opposite[k]].wait_recv

    for k in range(2):

        @pl.when(near[k][0])
        def _(k=k):
            halo(k)()
            for q in range(3):
                v = rowbuf[k, q].astype(F32)
                r = q if k == 0 else T + 3 + q
                for h in range(2):
                    xs[h, r * W + L : r * W + L + T] = v[:, h * 128 : h * 128 + 128]

    for k in range(2):

        @pl.when(near[2 + k][0])
        def _(k=k):
            halo(2 + k)()
            for c in range(3):
                v = colbuf[k, c].astype(F32)
                first = 3 * W + (L - 3 if k == 0 else L + T) + c
                for h in range(2):
                    xs[h, pl.ds(first, T, stride=W)] = v[:, h * 128 : h * 128 + 128]

    for k in range(4):

        @pl.when(near[4 + k][0])
        def _(k=k):
            halo(4 + k)()
            low, far = k >= 2, k % 2 == 1
            for c in range(3):
                v = corner[k, c].astype(F32)
                for q in range(3):
                    at = (T + 3 + q if low else q) * W + (L + T if far else L - 3) + c
                    s = q if low else 13 + q
                    for h in range(2):
                        xs[h, at : at + 1] = v[s : s + 1, h * 128 : h * 128 + 128]

    def spread_rows(r, carry):
        for h in range(2):
            for m in range(10):
                taps[h, m, r] = xs[h, pl.ds(r * W + (L - 3) + m, 8, stride=4)]
        return carry

    lax.fori_loop(0, T + 6, spread_rows, 0)

    loads[5].wait()
    loads[7].wait()

    def region_row(i, carry):
        def column(j, carry):
            for h in range(2):
                acc = jnp.broadcast_to(
                    dw_bias[:, h * 128 : h * 128 + 128].reshape(1, 1, 128), (8, 8, 128)
                )
                for b in range(7):
                    slab = taps[h, j + b, pl.ds(i * 8, 14)]
                    for a in range(7):
                        acc = acc + slab[a : a + 8] * wb[h, a * 7 + b]
                conv[h, pl.ds(pl.multiple_of(j * 64, 64), 64)] = acc.reshape(64, 128)
            return carry

        lax.fori_loop(0, 4, column, 0)
        for p in range(4):
            at = slice(p * 64, p * 64 + 64)
            x = [conv[h, at] for h in range(2)]
            mean = jnp.sum(x[0] + x[1], axis=-1, keepdims=True) * (1.0 / 256.0)
            x = [v - mean for v in x]
            var = jnp.sum(x[0] * x[0] + x[1] * x[1], axis=-1, keepdims=True) * (1.0 / 256.0)
            inv = lax.rsqrt(var + 1e-06)
            for h in range(2):
                lanes = slice(h * 128, h * 128 + 128)
                norm[at, lanes] = (x[h] * inv * gain[:, lanes] + nbias[:, lanes]).astype(BF16)
        n = norm[...]
        red = jnp.zeros((256, 256), F32)
        for f in range(4):
            part = slice(f * 256, f * 256 + 256)
            hid = gelu(dot(n, we[:, part]) + b_exp[:, part]).astype(BF16)
            red = red + dot(hid, wr[part, :])
        red = scale[...] * (red + b_red[...])
        for h in range(2):
            total = jnp.zeros((8, 128), F32)
            for j in range(4):
                v = red[j * 64 : j * 64 + 64, h * 128 : h * 128 + 128].reshape(8, 8, 128)
                v = (v + taps[h, j + 3, pl.ds(i * 8 + 3, 8)]).astype(BF16).astype(F32)
                total = total + jnp.sum(v, axis=0)
                for r in range(8):
                    block[h, pl.ds((i * 8 + r) * T + j, 8, stride=4)] = v[r]
            psum[h, pl.ds(pl.multiple_of(i * 8, 8), 8)] = total
        return carry

    lax.fori_loop(0, 4, region_row, 0)

    pooled = jnp.concatenate(
        [
            (psum[h, pl.ds(0, 16, stride=2)] + psum[h, pl.ds(1, 16, stride=2)]) * (1.0 / 64.0)
            for h in range(2)
        ],
        axis=1,
    ).astype(BF16)
    gath[col] = pooled
    gathers = []
    for d in range(1, n_col):
        c = pltpu.make_async_remote_copy(
            src_ref=gath.at[col],
            dst_ref=gath.at[col],
            send_sem=gsend.at[d - 1],
            recv_sem=grecv.at[d - 1],
            device_id=(row, lax.rem(col + d, n_col)),
            device_id_type=MESH,
        )
        c.start()
        gathers.append(c)
    loads[10].wait()
    loads[11].wait()
    loads[13].wait()
    queries = dot(pooled, wq[...]).astype(BF16).astype(F32)
    channel = lax.broadcasted_iota(jnp.int32, (8, 256), 1)
    head = lax.broadcasted_iota(jnp.int32, (8, 256), 0)
    own = ((channel >= head * 32) & (channel < head * 32 + 32)).astype(F32)
    spread = (queries[:, None, :] * own[None]).reshape(128, 256).astype(BF16)
    key = lax.broadcasted_iota(jnp.int32, (keys, 16 * n_col), 0)
    token = lax.broadcasted_iota(jnp.int32, (keys, 16 * n_col), 1)
    place = ((token % 16) // 4) * stride + (token // 16) * 4 + token % 4
    pick = (key == place).astype(F32).astype(BF16)
    for k, c in enumerate(sends):

        @pl.when(near[k][0])
        def _(c=c):
            c.wait_send()

    for c in gathers:
        c.wait()
    tokens = gath[...].reshape(16 * n_col, 256)
    ordered = dot(pick, tokens).astype(BF16)
    keyval = dot(ordered, wkv[...]).astype(BF16)
    scores = lax.dot_general(
        spread, keyval[:, :256], (((1,), (1,)), ((), ())), preferred_element_type=F32
    )
    scores = scores * (1.0 / 32.0**0.5) + bias[...].reshape(128, keys)
    top = jnp.max(scores, axis=-1, keepdims=True)
    e = jnp.exp(scores - top)
    attn = (e / jnp.sum(e, axis=-1, keepdims=True)).astype(BF16)
    ctx = dot(attn, keyval[:, 256:]).reshape(16, 8, 256)
    ctx = jnp.sum(ctx * own[None], axis=1).astype(BF16)
    psum_lift = dot(ctx, wo[...])
    for g in range(16):
        norm_row = psum_lift[g : g + 1]
        wb[0, g] = jnp.broadcast_to(norm_row[:, :128], (8, 128))
        wb[1, g] = jnp.broadcast_to(norm_row[:, 128:], (8, 128))

    def finish(r, carry):
        i = r // 8
        parts = []
        for h in range(2):
            v = block[h, pl.ds(pl.multiple_of(r * T, T), T)].reshape(4, 8, 128)
            parts.append((v + wb[h, pl.ds(i * 4, 4)]).reshape(T, 128))
        out[r] = jnp.concatenate(parts, axis=1).astype(BF16)
        return carry

    lax.fori_loop(0, T, finish, 0)


def shards(
    n_row,
    n_col,
    features,
    dw_kernel,
    dw_bias,
    norm_gain,
    norm_bias,
    w_expand,
    b_expand,
    w_reduce,
    b_reduce,
    layer_scale,
    w_query,
    w_keyval,
    rel_bias,
    w_out,
):
    lane = lambda v: v.reshape(1, -1)
    keys = 32 * n_col
    arrays = (
        features, dw_kernel, lane(dw_bias), lane(norm_gain), lane(norm_bias), w_expand,
        lane(b_expand), w_reduce, lane(b_reduce), lane(layer_scale), w_query, w_keyval,
        jnp.transpose(rel_bias, (1, 0, 2)), w_out,
    )
    hbm = pl.BlockSpec(memory_space=pltpu.HBM)
    vmem = pl.BlockSpec(memory_space=pltpu.VMEM)
    return pl.pallas_call(
        functools.partial(kernel, n_row, n_col),
        out_shape=jax.ShapeDtypeStruct(features.shape, BF16),
        in_specs=[hbm] * 14,
        out_specs=vmem,
        scratch_shapes=[pltpu.VMEM(v.shape, v.dtype) for v in arrays]
        + [
            pltpu.VMEM((4, 8, keys), F32),
            pltpu.VMEM((2, (T + 6) * W, 128), F32),
            pltpu.VMEM((2, 10, T + 6, 8, 128), F32),
            pltpu.VMEM((2, 49, 8, 128), F32),
            pltpu.VMEM((2, 256, 128), F32),
            pltpu.VMEM((256, 256), BF16),
            pltpu.VMEM((2, T * T, 128), F32),
            pltpu.VMEM((2, 32, 128), F32),
            pltpu.VMEM((16, 8, keys), F32),
            pltpu.VMEM((2, 3, T, 256), BF16),
            pltpu.VMEM((2, 3, T, 256), BF16),
            pltpu.VMEM((2, 3, T, 256), BF16),
            pltpu.VMEM((4, 3, 16, 256), BF16),
            pltpu.VMEM((n_col, 16, 256), BF16),
            pltpu.SemaphoreType.DMA((14,)),
            pltpu.SemaphoreType.DMA((8,)),
            pltpu.SemaphoreType.DMA((8,)),
            pltpu.SemaphoreType.DMA((n_col - 1,)),
            pltpu.SemaphoreType.DMA((n_col - 1,)),
        ],
        compiler_params=pltpu.CompilerParams(
            collective_id=0, has_side_effects=True, vmem_limit_bytes=63 * 1024 * 1024
        ),
    )(*arrays)


def solution(mesh):
    return jax.shard_map(
        functools.partial(shards, mesh.shape["row"], mesh.shape["col"]),
        mesh=mesh,
        in_specs=(P("row", "col", None),) + (P(),) * 13,
        out_specs=P("row", "col", None),
        check_vma=False,
    )
```

```python
import functools

import jax
import jax.numpy as jnp
from jax import lax
from jax.experimental import pallas as pl
from jax.experimental.pallas import tpu as pltpu
from jax.sharding import PartitionSpec as P

HEADS = 8
T = 32
W = 48
L = 8
MESH = pl.DeviceIdType.MESH
F32 = jnp.float32
BF16 = jnp.bfloat16


def dot(a, b):
    return jnp.dot(a, b, preferred_element_type=F32)


def gelu(x):
    size = jnp.abs(x)
    q = 1.0 + (0.3275911 * 0.7071067811865476) * size
    t = pl.reciprocal(q, approx=True)
    t = t * (2.0 - q * t)
    p = 0.5 * 1.061405429 * t - 0.5 * 1.453152027
    p = p * t + 0.5 * 1.421413741
    p = p * t - 0.5 * 0.284496736
    p = p * t + 0.5 * 0.254829592
    tail = (p * t) * jnp.exp2((x * x) * (-0.5 * 1.4426950408889634))
    return jnp.maximum(x, 0.0) - size * tail


def kernel(
    n_row,
    n_col,
    *refs,
):
    sources, out, local, rest = refs[:14], refs[14], refs[15:29], refs[29:]
    body(n_row, n_col, sources, out, local, *local, *rest)


def body(
    n_row,
    n_col,
    sources,
    out,
    local,
    feat,
    dw,
    dw_bias,
    gain,
    nbias,
    we,
    b_exp,
    wr,
    b_red,
    scale,
    wq,
    wkv,
    rel,
    wo,
    table,
    xs,
    taps,
    wb,
    conv,
    norm,
    block,
    psum,
    bias,
    stage,
    rowbuf,
    colbuf,
    corner,
    gath,
    wsem,
    send_sem,
    recv_sem,
    gsend,
    grecv,
):
    row = lax.axis_index("row")
    col = lax.axis_index("col")
    span = 4 * n_col
    stride = 2 * span
    keys = 4 * stride

    loads = [
        pltpu.make_async_copy(sources[k], local[k], wsem.at[k]) for k in range(len(local))
    ]
    for c in loads:
        c.start()

    up, down = row > 0, row < n_row - 1
    left, right = col > 0, col < n_col - 1
    both = jnp.logical_and
    near = (
        (up, -1, 0),
        (down, 1, 0),
        (left, 0, -1),
        (right, 0, 1),
        (both(up, left), -1, -1),
        (both(up, right), -1, 1),
        (both(down, left), 1, -1),
        (both(down, right), 1, 1),
    )
    barrier = pltpu.get_barrier_semaphore()
    for cond, dr, dc in near:
        if dr != 0:

            @pl.when(cond)
            def _(dr=dr, dc=dc):
                pl.semaphore_signal(
                    barrier, inc=1, device_id=(row + dr, col + dc), device_id_type=MESH
                )

    for d in range(1, n_col):
        pl.semaphore_signal(
            barrier, inc=1, device_id=(row, lax.rem(col + d, n_col)), device_id_type=MESH
        )

    for h in range(2):
        lanes = slice(h * 128, h * 128 + 128)
        xs[h, 0 : 3 * W] = jnp.zeros((3 * W, 128), F32)
        xs[h, 35 * W : 38 * W] = jnp.zeros((3 * W, 128), F32)

    def widen(r, carry):
        base = pl.multiple_of((r + 3) * W, 16)
        v = feat[r].astype(F32)
        zero = jnp.zeros((8, 128), F32)
        for h in range(2):
            xs[h, pl.ds(base, 8)] = zero
            xs[h, pl.ds(base + L, T)] = v[:, h * 128 : h * 128 + 128]
            xs[h, pl.ds(base + L + T, 8)] = zero
        return carry

    loads[0].wait()
    lax.fori_loop(0, T, widen, 0)
    for side, first in ((0, 0), (1, T - 3)):
        for c in range(3):
            for h in range(2):
                stage[side, c, :, h * 128 : h * 128 + 128] = xs[
                    h, pl.ds(3 * W + L + first + c, T, stride=W)
                ].astype(BF16)

    number = lambda c: c.astype(jnp.int32)
    across = 1 + number(left) + number(right)
    pl.semaphore_wait(barrier, n_col - 1 + across * (number(up) + number(down)))

    def remote(src, dst, k, dr, dc):
        return pltpu.make_async_remote_copy(
            src_ref=src,
            dst_ref=dst,
            send_sem=send_sem.at[k],
            recv_sem=recv_sem.at[k],
            device_id=(row + dr, col + dc),
            device_id_type=MESH,
        )

    plan = (
        (feat.at[0:3], rowbuf.at[1]),
        (feat.at[T - 3 : T], rowbuf.at[0]),
        (stage.at[0], colbuf.at[1]),
        (stage.at[1], colbuf.at[0]),
        (stage.at[0, :, 0:16], corner.at[3]),
        (stage.at[1, :, 0:16], corner.at[2]),
        (stage.at[0, :, 16:32], corner.at[1]),
        (stage.at[1, :, 16:32], corner.at[0]),
    )
    opposite = (1, 0, 3, 2, 7, 6, 5, 4)
    sends = [remote(s, d, k, near[k][1], near[k][2]) for k, (s, d) in enumerate(plan)]
    for k, c in enumerate(sends):

        @pl.when(near[k][0])
        def _(c=c):
            c.start()

    for k in (1, 2, 3, 4, 6, 8, 9, 12):
        loads[k].wait()
    for a in range(7):
        v = dw[a].astype(F32)
        for b in range(7):
            for h in range(2):
                wb[h, a * 7 + b] = jnp.broadcast_to(
                    v[b : b + 1, h * 128 : h * 128 + 128], (8, 128)
                )
    lane = lax.broadcasted_iota(jnp.int32, (8, keys), 1)
    valid = lax.rem(lane, stride) < span
    table[...] = jnp.zeros(table.shape, F32)
    for r in range(4):
        for k in range(4):
            width = 2 * span - 1
            table[r, :, k * stride : k * stride + width] = rel[k - r + 3]
        t = table[r]
        for c in range(4):
            shift = keys - (span - 1) + 4 * col + c
            moved = pltpu.roll(t, shift, 1)
            bias[r * 4 + c] = jnp.where(valid, moved, -1e30)

    def split_row(r, columns):
        for h in range(2):
            for m in columns:
                taps[h, m, r] = xs[h, pl.ds(r * W + (L - 3) + m, 8, stride=4)]

    def own_columns(r, carry):
        split_row(r, (3, 4, 5, 6))
        return carry

    lax.fori_loop(3, T + 3, own_columns, 0)

    def add(acc, h, i, m, b):
        slab = taps[h, m, pl.ds(i * 8, 14)]
        for a in range(7):
            acc = acc + slab[a : a + 8] * wb[h, a * 7 + b]
        return acc

    def inner(i, carry):
        def column(j, carry):
            for h in range(2):
                acc = jnp.broadcast_to(
                    dw_bias[:, h * 128 : h * 128 + 128].reshape(1, 1, 128), (8, 8, 128)
                )
                for m in range(3, 7):
                    acc = add(acc, h, i, m, m - j)
                conv[h, pl.ds((i * 4 + j) * 8, 8)] = acc
            return carry

        lax.fori_loop(0, 4, column, 0)
        return carry

    lax.fori_loop(1, 3, inner, 0)

    def halo(k):
        return sends[opposite[k]].wait_recv

    for k in range(2):

        @pl.when(near[k][0])
        def _(k=k):
            halo(k)()
            for q in range(3):
                v = rowbuf[k, q].astype(F32)
                r = q if k == 0 else T + 3 + q
                for h in range(2):
                    xs[h, r * W + L : r * W + L + T] = v[:, h * 128 : h * 128 + 128]

    for k in range(2):

        @pl.when(near[2 + k][0])
        def _(k=k):
            halo(2 + k)()
            for c in range(3):
                v = colbuf[k, c].astype(F32)
                first = 3 * W + (L - 3 if k == 0 else L + T) + c
                for h in range(2):
                    xs[h, pl.ds(first, T, stride=W)] = v[:, h * 128 : h * 128 + 128]

    for k in range(4):

        @pl.when(near[4 + k][0])
        def _(k=k):
            halo(4 + k)()
            low, far = k >= 2, k % 2 == 1
            for c in range(3):
                v = corner[k, c].astype(F32)
                for q in range(3):
                    at = (T + 3 + q if low else q) * W + (L + T if far else L - 3) + c
                    s = q if low else 13 + q
                    for h in range(2):
                        xs[h, at : at + 1] = v[s : s + 1, h * 128 : h * 128 + 128]

    def others(r, carry):
        split_row(r, (0, 1, 2, 7, 8, 9))
        return carry

    lax.fori_loop(3, T + 3, others, 0)
    for r in (0, 1, 2, T + 3, T + 4, T + 5):
        split_row(r, range(10))
    inner(0, 0)
    inner(3, 0)

    loads[5].wait()
    loads[7].wait()

    def region_row(i, carry):
        def column(j, carry):
            for h in range(2):
                acc = conv[h, pl.ds((i * 4 + j) * 8, 8)]
                for k in range(3):
                    b = k + 4 * lax.div(j + k, 3)
                    acc = add(acc, h, i, j + b, b)
                conv[h, pl.ds((i * 4 + j) * 8, 8)] = acc
            return carry

        lax.fori_loop(0, 4, column, 0)
        for p in range(4):
            at = slice(p * 64, p * 64 + 64)
            x = [conv[h, pl.ds(i * 32 + p * 8, 8)].reshape(64, 128) for h in range(2)]
            mean = jnp.sum(x[0] + x[1], axis=-1, keepdims=True) * (1.0 / 256.0)
            x = [v - mean for v in x]
            var = jnp.sum(x[0] * x[0] + x[1] * x[1], axis=-1, keepdims=True) * (1.0 / 256.0)
            inv = lax.rsqrt(var + 1e-06)
            for h in range(2):
                lanes = slice(h * 128, h * 128 + 128)
                norm[at, lanes] = (x[h] * inv * gain[:, lanes] + nbias[:, lanes]).astype(BF16)
        n = norm[...]
        red = jnp.zeros((256, 256), F32)
        for f in range(4):
            part = slice(f * 256, f * 256 + 256)
            hid = gelu(dot(n, we[:, part]) + b_exp[:, part]).astype(BF16)
            red = red + dot(hid, wr[part, :])
        red = scale[...] * (red + b_red[...])
        for h in range(2):
            total = jnp.zeros((8, 128), F32)
            for j in range(4):
                v = red[j * 64 : j * 64 + 64, h * 128 : h * 128 + 128].reshape(8, 8, 128)
                v = (v + taps[h, j + 3, pl.ds(i * 8 + 3, 8)]).astype(BF16).astype(F32)
                total = total + jnp.sum(v, axis=0)
                for r in range(8):
                    block[h, pl.ds((i * 8 + r) * T + j, 8, stride=4)] = v[r]
            psum[h, pl.ds(pl.multiple_of(i * 8, 8), 8)] = total
        return carry

    lax.fori_loop(0, 4, region_row, 0)

    pooled = jnp.concatenate(
        [
            (psum[h, pl.ds(0, 16, stride=2)] + psum[h, pl.ds(1, 16, stride=2)]) * (1.0 / 64.0)
            for h in range(2)
        ],
        axis=1,
    ).astype(BF16)
    gath[col] = pooled
    gathers = []
    for d in range(1, n_col):
        c = pltpu.make_async_remote_copy(
            src_ref=gath.at[col],
            dst_ref=gath.at[col],
            send_sem=gsend.at[d - 1],
            recv_sem=grecv.at[d - 1],
            device_id=(row, lax.rem(col + d, n_col)),
            device_id_type=MESH,
        )
        c.start()
        gathers.append(c)
    loads[10].wait()
    loads[11].wait()
    loads[13].wait()
    queries = dot(pooled, wq[...]).astype(BF16).astype(F32)
    channel = lax.broadcasted_iota(jnp.int32, (8, 256), 1)
    head = lax.broadcasted_iota(jnp.int32, (8, 256), 0)
    own = ((channel >= head * 32) & (channel < head * 32 + 32)).astype(F32)
    spread = (queries[:, None, :] * own[None]).reshape(128, 256).astype(BF16)
    key = lax.broadcasted_iota(jnp.int32, (keys, 16 * n_col), 0)
    token = lax.broadcasted_iota(jnp.int32, (keys, 16 * n_col), 1)
    place = ((token % 16) // 4) * stride + (token // 16) * 4 + token % 4
    pick = (key == place).astype(F32).astype(BF16)
    for k, c in enumerate(sends):

        @pl.when(near[k][0])
        def _(c=c):
            c.wait_send()

    for c in gathers:
        c.wait()
    tokens = gath[...].reshape(16 * n_col, 256)
    ordered = dot(pick, tokens).astype(BF16)
    keyval = dot(ordered, wkv[...]).astype(BF16)
    scores = lax.dot_general(
        spread, keyval[:, :256], (((1,), (1,)), ((), ())), preferred_element_type=F32
    )
    scores = scores * (1.0 / 32.0**0.5) + bias[...].reshape(128, keys)
    top = jnp.max(scores, axis=-1, keepdims=True)
    e = jnp.exp(scores - top)
    attn = (e / jnp.sum(e, axis=-1, keepdims=True)).astype(BF16)
    ctx = dot(attn, keyval[:, 256:]).reshape(16, 8, 256)
    ctx = jnp.sum(ctx * own[None], axis=1).astype(BF16)
    psum_lift = dot(ctx, wo[...])
    for g in range(16):
        norm_row = psum_lift[g : g + 1]
        wb[0, g] = jnp.broadcast_to(norm_row[:, :128], (8, 128))
        wb[1, g] = jnp.broadcast_to(norm_row[:, 128:], (8, 128))

    def finish(r, carry):
        i = r // 8
        parts = []
        for h in range(2):
            v = block[h, pl.ds(pl.multiple_of(r * T, T), T)].reshape(4, 8, 128)
            parts.append((v + wb[h, pl.ds(i * 4, 4)]).reshape(T, 128))
        out[r] = jnp.concatenate(parts, axis=1).astype(BF16)
        return carry

    lax.fori_loop(0, T, finish, 0)


def shards(
    n_row,
    n_col,
    features,
    dw_kernel,
    dw_bias,
    norm_gain,
    norm_bias,
    w_expand,
    b_expand,
    w_reduce,
    b_reduce,
    layer_scale,
    w_query,
    w_keyval,
    rel_bias,
    w_out,
):
    lane = lambda v: v.reshape(1, -1)
    keys = 32 * n_col
    arrays = (
        features, dw_kernel, lane(dw_bias), lane(norm_gain), lane(norm_bias), w_expand,
        lane(b_expand), w_reduce, lane(b_reduce), lane(layer_scale), w_query, w_keyval,
        jnp.transpose(rel_bias, (1, 0, 2)), w_out,
    )
    hbm = pl.BlockSpec(memory_space=pltpu.HBM)
    vmem = pl.BlockSpec(memory_space=pltpu.VMEM)
    return pl.pallas_call(
        functools.partial(kernel, n_row, n_col),
        out_shape=jax.ShapeDtypeStruct(features.shape, BF16),
        in_specs=[hbm] * 14,
        out_specs=vmem,
        scratch_shapes=[pltpu.VMEM(v.shape, v.dtype) for v in arrays]
        + [
            pltpu.VMEM((4, 8, keys), F32),
            pltpu.VMEM((2, (T + 6) * W, 128), F32),
            pltpu.VMEM((2, 10, T + 6, 8, 128), F32),
            pltpu.VMEM((2, 49, 8, 128), F32),
            pltpu.VMEM((2, 128, 8, 128), F32),
            pltpu.VMEM((256, 256), BF16),
            pltpu.VMEM((2, T * T, 128), F32),
            pltpu.VMEM((2, 32, 128), F32),
            pltpu.VMEM((16, 8, keys), F32),
            pltpu.VMEM((2, 3, T, 256), BF16),
            pltpu.VMEM((2, 3, T, 256), BF16),
            pltpu.VMEM((2, 3, T, 256), BF16),
            pltpu.VMEM((4, 3, 16, 256), BF16),
            pltpu.VMEM((n_col, 16, 256), BF16),
            pltpu.SemaphoreType.DMA((14,)),
            pltpu.SemaphoreType.DMA((8,)),
            pltpu.SemaphoreType.DMA((8,)),
            pltpu.SemaphoreType.DMA((n_col - 1,)),
            pltpu.SemaphoreType.DMA((n_col - 1,)),
        ],
        compiler_params=pltpu.CompilerParams(
            collective_id=0, has_side_effects=True, vmem_limit_bytes=40 * 1024 * 1024
        ),
    )(*[pltpu.with_memory_space_constraint(v, pltpu.HBM) for v in arrays])


def solution(mesh):
    return jax.shard_map(
        functools.partial(shards, mesh.shape["row"], mesh.shape["col"]),
        mesh=mesh,
        in_specs=(P("row", "col", None),) + (P(),) * 13,
        out_specs=P("row", "col", None),
        check_vma=False,
    )
```

```python
import functools

import jax
import jax.numpy as jnp
from jax import lax
from jax.experimental import pallas as pl
from jax.experimental.pallas import tpu as pltpu
from jax.sharding import PartitionSpec as P

HEADS = 8
T = 32
W = 48
L = 8
MESH = pl.DeviceIdType.MESH
F32 = jnp.float32
BF16 = jnp.bfloat16


def dot(a, b):
    return jnp.dot(a, b, preferred_element_type=F32)


def gelu(x):
    size = jnp.abs(x)
    q = 1.0 + (0.3275911 * 0.7071067811865476) * size
    t = pl.reciprocal(q, approx=True)
    t = t * (2.0 - q * t)
    p = 0.5 * 1.061405429 * t - 0.5 * 1.453152027
    p = p * t + 0.5 * 1.421413741
    p = p * t - 0.5 * 0.284496736
    p = p * t + 0.5 * 0.254829592
    tail = (p * t) * jnp.exp2((x * x) * (-0.5 * 1.4426950408889634))
    return jnp.maximum(x, 0.0) - size * tail


def kernel(
    n_row,
    n_col,
    *refs,
):
    sources, out, local, rest = refs[:14], refs[14], refs[15:29], refs[29:]
    body(n_row, n_col, sources, out, local, *local, *rest)


def body(
    n_row,
    n_col,
    sources,
    out,
    local,
    feat,
    dw,
    dw_bias,
    gain,
    nbias,
    we,
    b_exp,
    wr,
    b_red,
    scale,
    wq,
    wkv,
    rel,
    wo,
    table,
    xs,
    taps,
    wb,
    conv,
    norm,
    block,
    psum,
    bias,
    stage,
    rowbuf,
    colbuf,
    corner,
    gath,
    wsem,
    send_sem,
    recv_sem,
    gsend,
    grecv,
):
    row = lax.axis_index("row")
    col = lax.axis_index("col")
    span = 4 * n_col
    stride = 2 * span
    keys = 4 * stride

    loads = [
        pltpu.make_async_copy(sources[k], local[k], wsem.at[k]) for k in range(len(local))
    ]
    for c in loads:
        c.start()

    up, down = row > 0, row < n_row - 1
    left, right = col > 0, col < n_col - 1
    both = jnp.logical_and
    near = (
        (up, -1, 0),
        (down, 1, 0),
        (left, 0, -1),
        (right, 0, 1),
        (both(up, left), -1, -1),
        (both(up, right), -1, 1),
        (both(down, left), 1, -1),
        (both(down, right), 1, 1),
    )
    barrier = pltpu.get_barrier_semaphore()
    for cond, dr, dc in near:
        if dr != 0:

            @pl.when(cond)
            def _(dr=dr, dc=dc):
                pl.semaphore_signal(
                    barrier, inc=1, device_id=(row + dr, col + dc), device_id_type=MESH
                )

    for d in range(1, n_col):
        pl.semaphore_signal(
            barrier, inc=1, device_id=(row, lax.rem(col + d, n_col)), device_id_type=MESH
        )

    for h in range(2):
        lanes = slice(h * 128, h * 128 + 128)
        xs[h, 0 : 3 * W] = jnp.zeros((3 * W, 128), F32)
        xs[h, 35 * W : 38 * W] = jnp.zeros((3 * W, 128), F32)

    def widen(r, carry):
        base = pl.multiple_of((r + 3) * W, 16)
        v = feat[r].astype(F32)
        zero = jnp.zeros((8, 128), F32)
        for h in range(2):
            xs[h, pl.ds(base, 8)] = zero
            xs[h, pl.ds(base + L, T)] = v[:, h * 128 : h * 128 + 128]
            xs[h, pl.ds(base + L + T, 8)] = zero
        return carry

    loads[0].wait()
    lax.fori_loop(0, T, widen, 0, unroll=4)
    for side, first in ((0, 0), (1, T - 3)):
        for c in range(3):
            for h in range(2):
                stage[side, c, :, h * 128 : h * 128 + 128] = xs[
                    h, pl.ds(3 * W + L + first + c, T, stride=W)
                ].astype(BF16)

    number = lambda c: c.astype(jnp.int32)
    across = 1 + number(left) + number(right)
    pl.semaphore_wait(barrier, n_col - 1 + across * (number(up) + number(down)))

    def remote(src, dst, k, dr, dc):
        return pltpu.make_async_remote_copy(
            src_ref=src,
            dst_ref=dst,
            send_sem=send_sem.at[k],
            recv_sem=recv_sem.at[k],
            device_id=(row + dr, col + dc),
            device_id_type=MESH,
        )

    plan = (
        (feat.at[0:3], rowbuf.at[1]),
        (feat.at[T - 3 : T], rowbuf.at[0]),
        (stage.at[0], colbuf.at[1]),
        (stage.at[1], colbuf.at[0]),
        (stage.at[0, :, 0:16], corner.at[3]),
        (stage.at[1, :, 0:16], corner.at[2]),
        (stage.at[0, :, 16:32], corner.at[1]),
        (stage.at[1, :, 16:32], corner.at[0]),
    )
    opposite = (1, 0, 3, 2, 7, 6, 5, 4)
    sends = [remote(s, d, k, near[k][1], near[k][2]) for k, (s, d) in enumerate(plan)]
    for k, c in enumerate(sends):

        @pl.when(near[k][0])
        def _(c=c):
            c.start()

    for k in (1, 2, 3, 4, 6, 8, 9, 12):
        loads[k].wait()
    for a in range(7):
        v = dw[a].astype(F32)
        for b in range(7):
            for h in range(2):
                wb[h, a * 7 + b] = jnp.broadcast_to(
                    v[b : b + 1, h * 128 : h * 128 + 128], (8, 128)
                )
    lane = lax.broadcasted_iota(jnp.int32, (8, keys), 1)
    valid = lax.rem(lane, stride) < span
    table[...] = jnp.zeros(table.shape, F32)
    for r in range(4):
        for k in range(4):
            width = 2 * span - 1
            table[r, :, k * stride : k * stride + width] = rel[k - r + 3]
        t = table[r]
        for c in range(4):
            shift = keys - (span - 1) + 4 * col + c
            moved = pltpu.roll(t, shift, 1)
            bias[r * 4 + c] = jnp.where(valid, moved, -1e30)

    def split_row(r, columns):
        for h in range(2):
            for m in columns:
                taps[h, m, r] = xs[h, pl.ds(r * W + (L - 3) + m, 8, stride=4)]

    def own_columns(r, carry):
        split_row(r, (3, 4, 5, 6))
        return carry

    lax.fori_loop(3, T + 3, own_columns, 0, unroll=4)

    def add(acc, h, i, m, b):
        slab = taps[h, m, pl.ds(i * 8, 14)]
        for a in range(7):
            acc = acc + slab[a : a + 8] * wb[h, a * 7 + b]
        return acc

    def inner(i, carry):
        def column(j, carry):
            for h in range(2):
                acc = jnp.broadcast_to(
                    dw_bias[:, h * 128 : h * 128 + 128].reshape(1, 1, 128), (8, 8, 128)
                )
                for m in range(3, 7):
                    acc = add(acc, h, i, m, m - j)
                conv[h, pl.ds((i * 4 + j) * 8, 8)] = acc
            return carry

        lax.fori_loop(0, 4, column, 0)
        return carry

    lax.fori_loop(1, 3, inner, 0)

    def halo(k):
        return sends[opposite[k]].wait_recv

    for k in range(2):

        @pl.when(near[k][0])
        def _(k=k):
            halo(k)()
            for q in range(3):
                v = rowbuf[k, q].astype(F32)
                r = q if k == 0 else T + 3 + q
                for h in range(2):
                    xs[h, r * W + L : r * W + L + T] = v[:, h * 128 : h * 128 + 128]

    for k in range(2):

        @pl.when(near[2 + k][0])
        def _(k=k):
            halo(2 + k)()
            for c in range(3):
                v = colbuf[k, c].astype(F32)
                first = 3 * W + (L - 3 if k == 0 else L + T) + c
                for h in range(2):
                    xs[h, pl.ds(first, T, stride=W)] = v[:, h * 128 : h * 128 + 128]

    for k in range(4):

        @pl.when(near[4 + k][0])
        def _(k=k):
            halo(4 + k)()
            low, far = k >= 2, k % 2 == 1
            for c in range(3):
                v = corner[k, c].astype(F32)
                for q in range(3):
                    at = (T + 3 + q if low else q) * W + (L + T if far else L - 3) + c
                    s = q if low else 13 + q
                    for h in range(2):
                        xs[h, at : at + 1] = v[s : s + 1, h * 128 : h * 128 + 128]

    def others(r, carry):
        split_row(r, (0, 1, 2, 7, 8, 9))
        return carry

    lax.fori_loop(3, T + 3, others, 0, unroll=4)
    for r in (0, 1, 2, T + 3, T + 4, T + 5):
        split_row(r, range(10))
    inner(0, 0)
    inner(3, 0)

    loads[5].wait()
    loads[7].wait()

    def region_row(i, carry):
        def column(j, carry):
            for h in range(2):
                acc = conv[h, pl.ds((i * 4 + j) * 8, 8)]
                for k in range(3):
                    b = k + 4 * lax.div(j + k, 3)
                    acc = add(acc, h, i, j + b, b)
                conv[h, pl.ds((i * 4 + j) * 8, 8)] = acc
            return carry

        lax.fori_loop(0, 4, column, 0)
        for p in range(4):
            at = slice(p * 64, p * 64 + 64)
            x = [conv[h, pl.ds(i * 32 + p * 8, 8)].reshape(64, 128) for h in range(2)]
            mean = jnp.sum(x[0] + x[1], axis=-1, keepdims=True) * (1.0 / 256.0)
            x = [v - mean for v in x]
            var = jnp.sum(x[0] * x[0] + x[1] * x[1], axis=-1, keepdims=True) * (1.0 / 256.0)
            inv = lax.rsqrt(var + 1e-06)
            for h in range(2):
                lanes = slice(h * 128, h * 128 + 128)
                norm[at, lanes] = (x[h] * inv * gain[:, lanes] + nbias[:, lanes]).astype(BF16)
        n = norm[...]
        red = jnp.zeros((256, 256), F32)
        for f in range(4):
            part = slice(f * 256, f * 256 + 256)
            hid = gelu(dot(n, we[:, part]) + b_exp[:, part]).astype(BF16)
            red = red + dot(hid, wr[part, :])
        red = scale[...] * (red + b_red[...])
        for h in range(2):
            total = jnp.zeros((8, 128), F32)
            for j in range(4):
                v = red[j * 64 : j * 64 + 64, h * 128 : h * 128 + 128].reshape(8, 8, 128)
                v = (v + taps[h, j + 3, pl.ds(i * 8 + 3, 8)]).astype(BF16).astype(F32)
                total = total + jnp.sum(v, axis=0)
                for r in range(8):
                    block[h, pl.ds((i * 8 + r) * T + j, 8, stride=4)] = v[r]
            psum[h, pl.ds(pl.multiple_of(i * 8, 8), 8)] = total
        return carry

    lax.fori_loop(0, 4, region_row, 0)

    pooled = jnp.concatenate(
        [
            (psum[h, pl.ds(0, 16, stride=2)] + psum[h, pl.ds(1, 16, stride=2)]) * (1.0 / 64.0)
            for h in range(2)
        ],
        axis=1,
    ).astype(BF16)
    gath[col] = pooled
    gathers = []
    for d in range(1, n_col):
        c = pltpu.make_async_remote_copy(
            src_ref=gath.at[col],
            dst_ref=gath.at[col],
            send_sem=gsend.at[d - 1],
            recv_sem=grecv.at[d - 1],
            device_id=(row, lax.rem(col + d, n_col)),
            device_id_type=MESH,
        )
        c.start()
        gathers.append(c)
    loads[10].wait()
    loads[11].wait()
    loads[13].wait()
    queries = dot(pooled, wq[...]).astype(BF16).astype(F32)
    channel = lax.broadcasted_iota(jnp.int32, (8, 256), 1)
    head = lax.broadcasted_iota(jnp.int32, (8, 256), 0)
    own = ((channel >= head * 32) & (channel < head * 32 + 32)).astype(F32)
    spread = (queries[:, None, :] * own[None]).reshape(128, 256).astype(BF16)
    key = lax.broadcasted_iota(jnp.int32, (keys, 16 * n_col), 0)
    token = lax.broadcasted_iota(jnp.int32, (keys, 16 * n_col), 1)
    place = ((token % 16) // 4) * stride + (token // 16) * 4 + token % 4
    pick = (key == place).astype(F32).astype(BF16)
    for k, c in enumerate(sends):

        @pl.when(near[k][0])
        def _(c=c):
            c.wait_send()

    for c in gathers:
        c.wait()
    tokens = gath[...].reshape(16 * n_col, 256)
    ordered = dot(pick, tokens).astype(BF16)
    keyval = dot(ordered, wkv[...]).astype(BF16)
    scores = lax.dot_general(
        spread, keyval[:, :256], (((1,), (1,)), ((), ())), preferred_element_type=F32
    )
    scores = scores * (1.0 / 32.0**0.5) + bias[...].reshape(128, keys)
    top = jnp.max(scores, axis=-1, keepdims=True)
    e = jnp.exp(scores - top)
    attn = (e / jnp.sum(e, axis=-1, keepdims=True)).astype(BF16)
    ctx = dot(attn, keyval[:, 256:]).reshape(16, 8, 256)
    ctx = jnp.sum(ctx * own[None], axis=1).astype(BF16)
    psum_lift = dot(ctx, wo[...])
    for g in range(16):
        norm_row = psum_lift[g : g + 1]
        wb[0, g] = jnp.broadcast_to(norm_row[:, :128], (8, 128))
        wb[1, g] = jnp.broadcast_to(norm_row[:, 128:], (8, 128))

    def finish(r, carry):
        i = r // 8
        parts = []
        for h in range(2):
            v = block[h, pl.ds(pl.multiple_of(r * T, T), T)].reshape(4, 8, 128)
            parts.append((v + wb[h, pl.ds(i * 4, 4)]).reshape(T, 128))
        out[r] = jnp.concatenate(parts, axis=1).astype(BF16)
        return carry

    lax.fori_loop(0, T, finish, 0, unroll=4)


def shards(
    n_row,
    n_col,
    features,
    dw_kernel,
    dw_bias,
    norm_gain,
    norm_bias,
    w_expand,
    b_expand,
    w_reduce,
    b_reduce,
    layer_scale,
    w_query,
    w_keyval,
    rel_bias,
    w_out,
):
    lane = lambda v: v.reshape(1, -1)
    keys = 32 * n_col
    arrays = (
        features, dw_kernel, lane(dw_bias), lane(norm_gain), lane(norm_bias), w_expand,
        lane(b_expand), w_reduce, lane(b_reduce), lane(layer_scale), w_query, w_keyval,
        jnp.transpose(rel_bias, (1, 0, 2)), w_out,
    )
    hbm = pl.BlockSpec(memory_space=pltpu.HBM)
    vmem = pl.BlockSpec(memory_space=pltpu.VMEM)
    return pl.pallas_call(
        functools.partial(kernel, n_row, n_col),
        out_shape=jax.ShapeDtypeStruct(features.shape, BF16),
        in_specs=[hbm] * 14,
        out_specs=vmem,
        scratch_shapes=[pltpu.VMEM(v.shape, v.dtype) for v in arrays]
        + [
            pltpu.VMEM((4, 8, keys), F32),
            pltpu.VMEM((2, (T + 6) * W, 128), F32),
            pltpu.VMEM((2, 10, T + 6, 8, 128), F32),
            pltpu.VMEM((2, 49, 8, 128), F32),
            pltpu.VMEM((2, 128, 8, 128), F32),
            pltpu.VMEM((256, 256), BF16),
            pltpu.VMEM((2, T * T, 128), F32),
            pltpu.VMEM((2, 32, 128), F32),
            pltpu.VMEM((16, 8, keys), F32),
            pltpu.VMEM((2, 3, T, 256), BF16),
            pltpu.VMEM((2, 3, T, 256), BF16),
            pltpu.VMEM((2, 3, T, 256), BF16),
            pltpu.VMEM((4, 3, 16, 256), BF16),
            pltpu.VMEM((n_col, 16, 256), BF16),
            pltpu.SemaphoreType.DMA((14,)),
            pltpu.SemaphoreType.DMA((8,)),
            pltpu.SemaphoreType.DMA((8,)),
            pltpu.SemaphoreType.DMA((n_col - 1,)),
            pltpu.SemaphoreType.DMA((n_col - 1,)),
        ],
        compiler_params=pltpu.CompilerParams(
            collective_id=0, has_side_effects=True, vmem_limit_bytes=40 * 1024 * 1024
        ),
    )(*[pltpu.with_memory_space_constraint(v, pltpu.HBM) for v in arrays])


def solution(mesh):
    return jax.shard_map(
        functools.partial(shards, mesh.shape["row"], mesh.shape["col"]),
        mesh=mesh,
        in_specs=(P("row", "col", None),) + (P(),) * 13,
        out_specs=P("row", "col", None),
        check_vma=False,
    )
```

```python
import functools

import jax
import jax.numpy as jnp
from jax import lax
from jax.experimental import pallas as pl
from jax.experimental.pallas import tpu as pltpu
from jax.sharding import PartitionSpec as P

HEADS = 8
T = 32
W = 48
L = 8
MESH = pl.DeviceIdType.MESH
F32 = jnp.float32
BF16 = jnp.bfloat16


def dot(a, b):
    return jnp.dot(a, b, preferred_element_type=F32)


def gelu(x):
    size = jnp.abs(x)
    q = 1.0 + (0.3275911 * 0.7071067811865476) * size
    t = pl.reciprocal(q, approx=True)
    t = t * (2.0 - q * t)
    p = 0.5 * 1.061405429 * t - 0.5 * 1.453152027
    p = p * t + 0.5 * 1.421413741
    p = p * t - 0.5 * 0.284496736
    p = p * t + 0.5 * 0.254829592
    tail = (p * t) * jnp.exp2((x * x) * (-0.5 * 1.4426950408889634))
    return jnp.maximum(x, 0.0) - size * tail


def kernel(
    n_row,
    n_col,
    *refs,
):
    sources, out, local, rest = refs[:14], refs[14], refs[15:29], refs[29:]
    body(n_row, n_col, sources, out, local, *local, *rest)


def body(
    n_row,
    n_col,
    sources,
    out,
    local,
    feat,
    dw,
    dw_bias,
    gain,
    nbias,
    we,
    b_exp,
    wr,
    b_red,
    scale,
    wq,
    wkv,
    rel,
    wo,
    table,
    xs,
    taps,
    wb,
    conv,
    norm,
    block,
    psum,
    bias,
    stage,
    rowbuf,
    colbuf,
    corner,
    gath,
    wsem,
    send_sem,
    recv_sem,
    gsend,
    grecv,
):
    row = lax.axis_index("row")
    col = lax.axis_index("col")
    span = 4 * n_col
    stride = 2 * span
    keys = 4 * stride

    loads = [
        pltpu.make_async_copy(sources[k], local[k], wsem.at[k]) for k in range(len(local))
    ]
    for c in loads:
        c.start()

    up, down = row > 0, row < n_row - 1
    left, right = col > 0, col < n_col - 1
    both = jnp.logical_and
    near = (
        (up, -1, 0),
        (down, 1, 0),
        (left, 0, -1),
        (right, 0, 1),
        (both(up, left), -1, -1),
        (both(up, right), -1, 1),
        (both(down, left), 1, -1),
        (both(down, right), 1, 1),
    )
    barrier = pltpu.get_barrier_semaphore()
    for cond, dr, dc in near:
        if dr != 0:

            @pl.when(cond)
            def _(dr=dr, dc=dc):
                pl.semaphore_signal(
                    barrier, inc=1, device_id=(row + dr, col + dc), device_id_type=MESH
                )

    for d in range(1, n_col):
        pl.semaphore_signal(
            barrier, inc=1, device_id=(row, lax.rem(col + d, n_col)), device_id_type=MESH
        )

    for h in range(2):
        lanes = slice(h * 128, h * 128 + 128)
        xs[h, 0 : 3 * W] = jnp.zeros((3 * W, 128), F32)
        xs[h, 35 * W : 38 * W] = jnp.zeros((3 * W, 128), F32)

    def widen(r, carry):
        base = pl.multiple_of((r + 3) * W, 16)
        v = feat[r].astype(F32)
        zero = jnp.zeros((8, 128), F32)
        for h in range(2):
            xs[h, pl.ds(base, 8)] = zero
            xs[h, pl.ds(base + L, T)] = v[:, h * 128 : h * 128 + 128]
            xs[h, pl.ds(base + L + T, 8)] = zero
        return carry

    loads[0].wait()
    lax.fori_loop(0, T, widen, 0, unroll=4)
    for side, first in ((0, 0), (1, T - 3)):
        for c in range(3):
            for h in range(2):
                stage[side, c, :, h * 128 : h * 128 + 128] = xs[
                    h, pl.ds(3 * W + L + first + c, T, stride=W)
                ].astype(BF16)

    number = lambda c: c.astype(jnp.int32)
    across = 1 + number(left) + number(right)
    pl.semaphore_wait(barrier, n_col - 1 + across * (number(up) + number(down)))

    def remote(src, dst, k, dr, dc):
        return pltpu.make_async_remote_copy(
            src_ref=src,
            dst_ref=dst,
            send_sem=send_sem.at[k],
            recv_sem=recv_sem.at[k],
            device_id=(row + dr, col + dc),
            device_id_type=MESH,
        )

    plan = (
        (feat.at[0:3], rowbuf.at[1]),
        (feat.at[T - 3 : T], rowbuf.at[0]),
        (stage.at[0], colbuf.at[1]),
        (stage.at[1], colbuf.at[0]),
        (stage.at[0, :, 0:16], corner.at[3]),
        (stage.at[1, :, 0:16], corner.at[2]),
        (stage.at[0, :, 16:32], corner.at[1]),
        (stage.at[1, :, 16:32], corner.at[0]),
    )
    opposite = (1, 0, 3, 2, 7, 6, 5, 4)
    sends = [remote(s, d, k, near[k][1], near[k][2]) for k, (s, d) in enumerate(plan)]
    for k, c in enumerate(sends):

        @pl.when(near[k][0])
        def _(c=c):
            c.start()

    for k in (1, 2, 3, 4, 6, 8, 9, 12):
        loads[k].wait()
    for a in range(7):
        v = dw[a].astype(F32)
        for b in range(7):
            for h in range(2):
                wb[h, a * 7 + b] = jnp.broadcast_to(
                    v[b : b + 1, h * 128 : h * 128 + 128], (8, 128)
                )
    lane = lax.broadcasted_iota(jnp.int32, (8, keys), 1)
    valid = lax.rem(lane, stride) < span
    table[...] = jnp.zeros(table.shape, F32)
    for r in range(4):
        for k in range(4):
            width = 2 * span - 1
            table[r, :, k * stride : k * stride + width] = rel[k - r + 3]
        t = table[r]
        for c in range(4):
            shift = keys - (span - 1) + 4 * col + c
            moved = pltpu.roll(t, shift, 1)
            bias[r * 4 + c] = jnp.where(valid, moved, -1e30)

    def split_row(r, columns):
        for h in range(2):
            for m in columns:
                taps[h, m, r] = xs[h, pl.ds(r * W + (L - 3) + m, 8, stride=4)]

    def own_columns(r, carry):
        split_row(r, (3, 4, 5, 6))
        return carry

    lax.fori_loop(3, T + 3, own_columns, 0, unroll=4)

    def add(acc, h, i, m, b):
        slab = taps[h, m, pl.ds(i * 8, 14)]
        for a in range(7):
            acc = acc + slab[a : a + 8] * wb[h, a * 7 + b]
        return acc

    def inner(i, carry):
        def column(j, carry):
            for h in range(2):
                acc = jnp.broadcast_to(
                    dw_bias[:, h * 128 : h * 128 + 128].reshape(1, 1, 128), (8, 8, 128)
                )
                for m in range(3, 7):
                    acc = add(acc, h, i, m, m - j)
                conv[h, pl.ds((i * 4 + j) * 8, 8)] = acc
            return carry

        lax.fori_loop(0, 4, column, 0, unroll=2)
        return carry

    lax.fori_loop(1, 3, inner, 0)

    def halo(k):
        return sends[opposite[k]].wait_recv

    for k in range(2):

        @pl.when(near[k][0])
        def _(k=k):
            halo(k)()
            for q in range(3):
                v = rowbuf[k, q].astype(F32)
                r = q if k == 0 else T + 3 + q
                for h in range(2):
                    xs[h, r * W + L : r * W + L + T] = v[:, h * 128 : h * 128 + 128]

    for k in range(2):

        @pl.when(near[2 + k][0])
        def _(k=k):
            halo(2 + k)()
            for c in range(3):
                v = colbuf[k, c].astype(F32)
                first = 3 * W + (L - 3 if k == 0 else L + T) + c
                for h in range(2):
                    xs[h, pl.ds(first, T, stride=W)] = v[:, h * 128 : h * 128 + 128]

    for k in range(4):

        @pl.when(near[4 + k][0])
        def _(k=k):
            halo(4 + k)()
            low, far = k >= 2, k % 2 == 1
            for c in range(3):
                v = corner[k, c].astype(F32)
                for q in range(3):
                    at = (T + 3 + q if low else q) * W + (L + T if far else L - 3) + c
                    s = q if low else 13 + q
                    for h in range(2):
                        xs[h, at : at + 1] = v[s : s + 1, h * 128 : h * 128 + 128]

    def others(r, carry):
        split_row(r, (0, 1, 2, 7, 8, 9))
        return carry

    lax.fori_loop(3, T + 3, others, 0, unroll=4)
    for r in (0, 1, 2, T + 3, T + 4, T + 5):
        split_row(r, range(10))
    inner(0, 0)
    inner(3, 0)

    loads[5].wait()
    loads[7].wait()

    def region_row(i, carry):
        def column(j, carry):
            for h in range(2):
                acc = conv[h, pl.ds((i * 4 + j) * 8, 8)]
                for k in range(3):
                    b = k + 4 * lax.div(j + k, 3)
                    acc = add(acc, h, i, j + b, b)
                conv[h, pl.ds((i * 4 + j) * 8, 8)] = acc
            return carry

        lax.fori_loop(0, 4, column, 0, unroll=4)
        for p in range(4):
            at = slice(p * 64, p * 64 + 64)
            x = [conv[h, pl.ds(i * 32 + p * 8, 8)].reshape(64, 128) for h in range(2)]
            mean = jnp.sum(x[0] + x[1], axis=-1, keepdims=True) * (1.0 / 256.0)
            x = [v - mean for v in x]
            var = jnp.sum(x[0] * x[0] + x[1] * x[1], axis=-1, keepdims=True) * (1.0 / 256.0)
            inv = lax.rsqrt(var + 1e-06)
            for h in range(2):
                lanes = slice(h * 128, h * 128 + 128)
                norm[at, lanes] = (x[h] * inv * gain[:, lanes] + nbias[:, lanes]).astype(BF16)
        n = norm[...]
        red = jnp.zeros((256, 256), F32)
        for f in range(4):
            part = slice(f * 256, f * 256 + 256)
            hid = gelu(dot(n, we[:, part]) + b_exp[:, part]).astype(BF16)
            red = red + dot(hid, wr[part, :])
        red = scale[...] * (red + b_red[...])
        for h in range(2):
            total = jnp.zeros((8, 128), F32)
            for j in range(4):
                v = red[j * 64 : j * 64 + 64, h * 128 : h * 128 + 128].reshape(8, 8, 128)
                v = (v + taps[h, j + 3, pl.ds(i * 8 + 3, 8)]).astype(BF16).astype(F32)
                total = total + jnp.sum(v, axis=0)
                for r in range(8):
                    block[h, pl.ds((i * 8 + r) * T + j, 8, stride=4)] = v[r]
            psum[h, pl.ds(pl.multiple_of(i * 8, 8), 8)] = total
        return carry

    lax.fori_loop(0, 4, region_row, 0)

    pooled = jnp.concatenate(
        [
            (psum[h, pl.ds(0, 16, stride=2)] + psum[h, pl.ds(1, 16, stride=2)]) * (1.0 / 64.0)
            for h in range(2)
        ],
        axis=1,
    ).astype(BF16)
    gath[col] = pooled
    gathers = []
    for d in range(1, n_col):
        c = pltpu.make_async_remote_copy(
            src_ref=gath.at[col],
            dst_ref=gath.at[col],
            send_sem=gsend.at[d - 1],
            recv_sem=grecv.at[d - 1],
            device_id=(row, lax.rem(col + d, n_col)),
            device_id_type=MESH,
        )
        c.start()
        gathers.append(c)
    loads[10].wait()
    loads[11].wait()
    loads[13].wait()
    queries = dot(pooled, wq[...]).astype(BF16).astype(F32)
    channel = lax.broadcasted_iota(jnp.int32, (8, 256), 1)
    head = lax.broadcasted_iota(jnp.int32, (8, 256), 0)
    own = ((channel >= head * 32) & (channel < head * 32 + 32)).astype(F32)
    spread = (queries[:, None, :] * own[None]).reshape(128, 256).astype(BF16)
    key = lax.broadcasted_iota(jnp.int32, (keys, 16 * n_col), 0)
    token = lax.broadcasted_iota(jnp.int32, (keys, 16 * n_col), 1)
    place = ((token % 16) // 4) * stride + (token // 16) * 4 + token % 4
    pick = (key == place).astype(F32).astype(BF16)
    for k, c in enumerate(sends):

        @pl.when(near[k][0])
        def _(c=c):
            c.wait_send()

    for c in gathers:
        c.wait()
    tokens = gath[...].reshape(16 * n_col, 256)
    ordered = dot(pick, tokens).astype(BF16)
    keyval = dot(ordered, wkv[...]).astype(BF16)
    scores = lax.dot_general(
        spread, keyval[:, :256], (((1,), (1,)), ((), ())), preferred_element_type=F32
    )
    scores = scores * (1.0 / 32.0**0.5) + bias[...].reshape(128, keys)
    top = jnp.max(scores, axis=-1, keepdims=True)
    e = jnp.exp(scores - top)
    attn = (e / jnp.sum(e, axis=-1, keepdims=True)).astype(BF16)
    ctx = dot(attn, keyval[:, 256:]).reshape(16, 8, 256)
    ctx = jnp.sum(ctx * own[None], axis=1).astype(BF16)
    psum_lift = dot(ctx, wo[...])
    for g in range(16):
        norm_row = psum_lift[g : g + 1]
        wb[0, g] = jnp.broadcast_to(norm_row[:, :128], (8, 128))
        wb[1, g] = jnp.broadcast_to(norm_row[:, 128:], (8, 128))

    def finish(r, carry):
        i = r // 8
        parts = []
        for h in range(2):
            v = block[h, pl.ds(pl.multiple_of(r * T, T), T)].reshape(4, 8, 128)
            parts.append((v + wb[h, pl.ds(i * 4, 4)]).reshape(T, 128))
        out[r] = jnp.concatenate(parts, axis=1).astype(BF16)
        return carry

    lax.fori_loop(0, T, finish, 0, unroll=4)


def shards(
    n_row,
    n_col,
    features,
    dw_kernel,
    dw_bias,
    norm_gain,
    norm_bias,
    w_expand,
    b_expand,
    w_reduce,
    b_reduce,
    layer_scale,
    w_query,
    w_keyval,
    rel_bias,
    w_out,
):
    lane = lambda v: v.reshape(1, -1)
    keys = 32 * n_col
    arrays = (
        features, dw_kernel, lane(dw_bias), lane(norm_gain), lane(norm_bias), w_expand,
        lane(b_expand), w_reduce, lane(b_reduce), lane(layer_scale), w_query, w_keyval,
        jnp.transpose(rel_bias, (1, 0, 2)), w_out,
    )
    hbm = pl.BlockSpec(memory_space=pltpu.HBM)
    vmem = pl.BlockSpec(memory_space=pltpu.VMEM)
    return pl.pallas_call(
        functools.partial(kernel, n_row, n_col),
        out_shape=jax.ShapeDtypeStruct(features.shape, BF16),
        in_specs=[hbm] * 14,
        out_specs=vmem,
        scratch_shapes=[pltpu.VMEM(v.shape, v.dtype) for v in arrays]
        + [
            pltpu.VMEM((4, 8, keys), F32),
            pltpu.VMEM((2, (T + 6) * W, 128), F32),
            pltpu.VMEM((2, 10, T + 6, 8, 128), F32),
            pltpu.VMEM((2, 49, 8, 128), F32),
            pltpu.VMEM((2, 128, 8, 128), F32),
            pltpu.VMEM((256, 256), BF16),
            pltpu.VMEM((2, T * T, 128), F32),
            pltpu.VMEM((2, 32, 128), F32),
            pltpu.VMEM((16, 8, keys), F32),
            pltpu.VMEM((2, 3, T, 256), BF16),
            pltpu.VMEM((2, 3, T, 256), BF16),
            pltpu.VMEM((2, 3, T, 256), BF16),
            pltpu.VMEM((4, 3, 16, 256), BF16),
            pltpu.VMEM((n_col, 16, 256), BF16),
            pltpu.SemaphoreType.DMA((14,)),
            pltpu.SemaphoreType.DMA((8,)),
            pltpu.SemaphoreType.DMA((8,)),
            pltpu.SemaphoreType.DMA((n_col - 1,)),
            pltpu.SemaphoreType.DMA((n_col - 1,)),
        ],
        compiler_params=pltpu.CompilerParams(
            collective_id=0, has_side_effects=True, vmem_limit_bytes=40 * 1024 * 1024
        ),
    )(*[pltpu.with_memory_space_constraint(v, pltpu.HBM) for v in arrays])


def solution(mesh):
    return jax.shard_map(
        functools.partial(shards, mesh.shape["row"], mesh.shape["col"]),
        mesh=mesh,
        in_specs=(P("row", "col", None),) + (P(),) * 13,
        out_specs=P("row", "col", None),
        check_vma=False,
    )
```

```python
import functools

import jax
import jax.numpy as jnp
from jax import lax
from jax.experimental import pallas as pl
from jax.experimental.pallas import tpu as pltpu
from jax.sharding import PartitionSpec as P

HEADS = 8
T = 32
W = 48
L = 8
MESH = pl.DeviceIdType.MESH
F32 = jnp.float32
BF16 = jnp.bfloat16


def dot(a, b):
    return jnp.dot(a, b, preferred_element_type=F32)


def gelu(x):
    size = jnp.abs(x)
    q = 1.0 + (0.3275911 * 0.7071067811865476) * size
    t = pl.reciprocal(q, approx=True)
    t = t * (2.0 - q * t)
    p = 0.5 * 1.061405429 * t - 0.5 * 1.453152027
    p = p * t + 0.5 * 1.421413741
    p = p * t - 0.5 * 0.284496736
    p = p * t + 0.5 * 0.254829592
    tail = (p * t) * jnp.exp2((x * x) * (-0.5 * 1.4426950408889634))
    return jnp.maximum(x, 0.0) - size * tail


def kernel(
    n_row,
    n_col,
    *refs,
):
    sources, out, local, rest = refs[:14], refs[14], refs[15:29], refs[29:]
    body(n_row, n_col, sources, out, local, *local, *rest)


def body(
    n_row,
    n_col,
    sources,
    out,
    local,
    feat,
    dw,
    dw_bias,
    gain,
    nbias,
    we,
    b_exp,
    wr,
    b_red,
    scale,
    wq,
    wkv,
    rel,
    wo,
    table,
    xs,
    taps,
    wb,
    conv,
    norm,
    block,
    psum,
    bias,
    stage,
    rowbuf,
    colbuf,
    corner,
    gath,
    wsem,
    send_sem,
    recv_sem,
    gsend,
    grecv,
):
    row = lax.axis_index("row")
    col = lax.axis_index("col")
    span = 4 * n_col
    stride = 2 * span
    keys = 4 * stride

    loads = [
        pltpu.make_async_copy(sources[k], local[k], wsem.at[k]) for k in range(len(local))
    ]
    for c in loads:
        c.start()

    up, down = row > 0, row < n_row - 1
    left, right = col > 0, col < n_col - 1
    both = jnp.logical_and
    near = (
        (up, -1, 0),
        (down, 1, 0),
        (left, 0, -1),
        (right, 0, 1),
        (both(up, left), -1, -1),
        (both(up, right), -1, 1),
        (both(down, left), 1, -1),
        (both(down, right), 1, 1),
    )
    barrier = pltpu.get_barrier_semaphore()
    for cond, dr, dc in near:
        if dr != 0:

            @pl.when(cond)
            def _(dr=dr, dc=dc):
                pl.semaphore_signal(
                    barrier, inc=1, device_id=(row + dr, col + dc), device_id_type=MESH
                )

    for d in range(1, n_col):
        pl.semaphore_signal(
            barrier, inc=1, device_id=(row, lax.rem(col + d, n_col)), device_id_type=MESH
        )

    for h in range(2):
        lanes = slice(h * 128, h * 128 + 128)
        xs[h, 0 : 3 * W] = jnp.zeros((3 * W, 128), F32)
        xs[h, 35 * W : 38 * W] = jnp.zeros((3 * W, 128), F32)

    def widen(r, carry):
        base = pl.multiple_of((r + 3) * W, 16)
        v = feat[r].astype(F32)
        zero = jnp.zeros((8, 128), F32)
        for h in range(2):
            xs[h, pl.ds(base, 8)] = zero
            xs[h, pl.ds(base + L, T)] = v[:, h * 128 : h * 128 + 128]
            xs[h, pl.ds(base + L + T, 8)] = zero
        return carry

    loads[0].wait()
    lax.fori_loop(0, T, widen, 0, unroll=4)
    for side, first in ((0, 0), (1, T - 3)):
        for c in range(3):
            for h in range(2):
                stage[side, c, :, h * 128 : h * 128 + 128] = xs[
                    h, pl.ds(3 * W + L + first + c, T, stride=W)
                ].astype(BF16)

    number = lambda c: c.astype(jnp.int32)
    across = 1 + number(left) + number(right)
    pl.semaphore_wait(barrier, n_col - 1 + across * (number(up) + number(down)))

    def remote(src, dst, k, dr, dc):
        return pltpu.make_async_remote_copy(
            src_ref=src,
            dst_ref=dst,
            send_sem=send_sem.at[k],
            recv_sem=recv_sem.at[k],
            device_id=(row + dr, col + dc),
            device_id_type=MESH,
        )

    plan = (
        (feat.at[0:3], rowbuf.at[1]),
        (feat.at[T - 3 : T], rowbuf.at[0]),
        (stage.at[0], colbuf.at[1]),
        (stage.at[1], colbuf.at[0]),
        (stage.at[0, :, 0:16], corner.at[3]),
        (stage.at[1, :, 0:16], corner.at[2]),
        (stage.at[0, :, 16:32], corner.at[1]),
        (stage.at[1, :, 16:32], corner.at[0]),
    )
    opposite = (1, 0, 3, 2, 7, 6, 5, 4)
    sends = [remote(s, d, k, near[k][1], near[k][2]) for k, (s, d) in enumerate(plan)]
    for k, c in enumerate(sends):

        @pl.when(near[k][0])
        def _(c=c):
            c.start()

    for k in (1, 2, 3, 4, 6, 8, 9, 12):
        loads[k].wait()
    for a in range(7):
        v = dw[a].astype(F32)
        for b in range(7):
            for h in range(2):
                wb[h, a * 7 + b] = jnp.broadcast_to(
                    v[b : b + 1, h * 128 : h * 128 + 128], (8, 128)
                )
    lane = lax.broadcasted_iota(jnp.int32, (8, keys), 1)
    valid = lax.rem(lane, stride) < span
    table[...] = jnp.zeros(table.shape, F32)
    for r in range(4):
        for k in range(4):
            width = 2 * span - 1
            table[r, :, k * stride : k * stride + width] = rel[k - r + 3]
        t = table[r]
        for c in range(4):
            shift = keys - (span - 1) + 4 * col + c
            moved = pltpu.roll(t, shift, 1)
            bias[r * 4 + c] = jnp.where(valid, moved, -1e30)

    def split_row(r, columns):
        for h in range(2):
            for m in columns:
                taps[h, m, r] = xs[h, pl.ds(r * W + (L - 3) + m, 8, stride=4)]

    def own_columns(r, carry):
        split_row(r, (3, 4, 5, 6))
        return carry

    lax.fori_loop(3, T + 3, own_columns, 0, unroll=4)

    def add(acc, h, i, m, b):
        slab = taps[h, m, pl.ds(i * 8, 14)]
        for a in range(7):
            acc = acc + slab[a : a + 8] * wb[h, a * 7 + b]
        return acc

    def inner(i, carry):
        def column(j, carry):
            for h in range(2):
                acc = jnp.broadcast_to(
                    dw_bias[:, h * 128 : h * 128 + 128].reshape(1, 1, 128), (8, 8, 128)
                )
                for m in range(3, 7):
                    acc = add(acc, h, i, m, m - j)
                conv[h, pl.ds((i * 4 + j) * 8, 8)] = acc
            return carry

        lax.fori_loop(0, 4, column, 0, unroll=2)
        return carry

    lax.fori_loop(1, 3, inner, 0)

    def halo(k):
        return sends[opposite[k]].wait_recv

    for k in range(2):

        @pl.when(near[k][0])
        def _(k=k):
            halo(k)()
            for q in range(3):
                v = rowbuf[k, q].astype(F32)
                r = q if k == 0 else T + 3 + q
                for h in range(2):
                    xs[h, r * W + L : r * W + L + T] = v[:, h * 128 : h * 128 + 128]

    for k in range(2):

        @pl.when(near[2 + k][0])
        def _(k=k):
            halo(2 + k)()
            for c in range(3):
                v = colbuf[k, c].astype(F32)
                first = 3 * W + (L - 3 if k == 0 else L + T) + c
                for h in range(2):
                    xs[h, pl.ds(first, T, stride=W)] = v[:, h * 128 : h * 128 + 128]

    for k in range(4):

        @pl.when(near[4 + k][0])
        def _(k=k):
            halo(4 + k)()
            low, far = k >= 2, k % 2 == 1
            for c in range(3):
                v = corner[k, c].astype(F32)
                for q in range(3):
                    at = (T + 3 + q if low else q) * W + (L + T if far else L - 3) + c
                    s = q if low else 13 + q
                    for h in range(2):
                        xs[h, at : at + 1] = v[s : s + 1, h * 128 : h * 128 + 128]

    def others(r, carry):
        split_row(r, (0, 1, 2, 7, 8, 9))
        return carry

    lax.fori_loop(3, T + 3, others, 0, unroll=4)
    for r in (0, 1, 2, T + 3, T + 4, T + 5):
        split_row(r, range(10))
    inner(0, 0)
    inner(3, 0)

    loads[5].wait()
    loads[7].wait()

    def region_row(i, carry):
        def column(j, carry):
            for h in range(2):
                acc = conv[h, pl.ds((i * 4 + j) * 8, 8)]
                for k in range(3):
                    b = k + 4 * lax.div(j + k, 3)
                    acc = add(acc, h, i, j + b, b)
                conv[h, pl.ds((i * 4 + j) * 8, 8)] = acc
            return carry

        lax.fori_loop(0, 4, column, 0, unroll=4)
        for p in range(4):
            at = slice(p * 64, p * 64 + 64)
            x = [conv[h, pl.ds(i * 32 + p * 8, 8)].reshape(64, 128) for h in range(2)]
            mean = jnp.sum(x[0] + x[1], axis=-1, keepdims=True) * (1.0 / 256.0)
            x = [v - mean for v in x]
            var = jnp.sum(x[0] * x[0] + x[1] * x[1], axis=-1, keepdims=True) * (1.0 / 256.0)
            inv = lax.rsqrt(var + 1e-06)
            for h in range(2):
                lanes = slice(h * 128, h * 128 + 128)
                norm[at, lanes] = (x[h] * inv * gain[:, lanes] + nbias[:, lanes]).astype(BF16)
        n = norm[...]
        red = jnp.zeros((256, 256), F32)
        for f in range(4):
            part = slice(f * 256, f * 256 + 256)
            hid = gelu(dot(n, we[:, part]) + b_exp[:, part]).astype(BF16)
            red = red + dot(hid, wr[part, :])
        red = scale[...] * (red + b_red[...])
        for h in range(2):
            total = jnp.zeros((8, 128), F32)
            for j in range(4):
                v = red[j * 64 : j * 64 + 64, h * 128 : h * 128 + 128].reshape(8, 8, 128)
                v = (v + taps[h, j + 3, pl.ds(i * 8 + 3, 8)]).astype(BF16).astype(F32)
                total = total + jnp.sum(v, axis=0)
                for r in range(8):
                    block[h, pl.ds((i * 8 + r) * T + j, 8, stride=4)] = v[r]
            psum[h, pl.ds(pl.multiple_of(i * 8, 8), 8)] = total
        return carry

    lax.fori_loop(0, 4, region_row, 0, unroll=2)

    pooled = jnp.concatenate(
        [
            (psum[h, pl.ds(0, 16, stride=2)] + psum[h, pl.ds(1, 16, stride=2)]) * (1.0 / 64.0)
            for h in range(2)
        ],
        axis=1,
    ).astype(BF16)
    gath[col] = pooled
    gathers = []
    for d in range(1, n_col):
        c = pltpu.make_async_remote_copy(
            src_ref=gath.at[col],
            dst_ref=gath.at[col],
            send_sem=gsend.at[d - 1],
            recv_sem=grecv.at[d - 1],
            device_id=(row, lax.rem(col + d, n_col)),
            device_id_type=MESH,
        )
        c.start()
        gathers.append(c)
    loads[10].wait()
    loads[11].wait()
    loads[13].wait()
    queries = dot(pooled, wq[...]).astype(BF16).astype(F32)
    channel = lax.broadcasted_iota(jnp.int32, (8, 256), 1)
    head = lax.broadcasted_iota(jnp.int32, (8, 256), 0)
    own = ((channel >= head * 32) & (channel < head * 32 + 32)).astype(F32)
    spread = (queries[:, None, :] * own[None]).reshape(128, 256).astype(BF16)
    key = lax.broadcasted_iota(jnp.int32, (keys, 16 * n_col), 0)
    token = lax.broadcasted_iota(jnp.int32, (keys, 16 * n_col), 1)
    place = ((token % 16) // 4) * stride + (token // 16) * 4 + token % 4
    pick = (key == place).astype(F32).astype(BF16)
    for k, c in enumerate(sends):

        @pl.when(near[k][0])
        def _(c=c):
            c.wait_send()

    for c in gathers:
        c.wait()
    tokens = gath[...].reshape(16 * n_col, 256)
    ordered = dot(pick, tokens).astype(BF16)
    keyval = dot(ordered, wkv[...]).astype(BF16)
    scores = lax.dot_general(
        spread, keyval[:, :256], (((1,), (1,)), ((), ())), preferred_element_type=F32
    )
    scores = scores * (1.0 / 32.0**0.5) + bias[...].reshape(128, keys)
    top = jnp.max(scores, axis=-1, keepdims=True)
    e = jnp.exp(scores - top)
    attn = (e / jnp.sum(e, axis=-1, keepdims=True)).astype(BF16)
    ctx = dot(attn, keyval[:, 256:]).reshape(16, 8, 256)
    ctx = jnp.sum(ctx * own[None], axis=1).astype(BF16)
    psum_lift = dot(ctx, wo[...])
    for g in range(16):
        norm_row = psum_lift[g : g + 1]
        wb[0, g] = jnp.broadcast_to(norm_row[:, :128], (8, 128))
        wb[1, g] = jnp.broadcast_to(norm_row[:, 128:], (8, 128))

    def finish(r, carry):
        i = r // 8
        parts = []
        for h in range(2):
            v = block[h, pl.ds(pl.multiple_of(r * T, T), T)].reshape(4, 8, 128)
            parts.append((v + wb[h, pl.ds(i * 4, 4)]).reshape(T, 128))
        out[r] = jnp.concatenate(parts, axis=1).astype(BF16)
        return carry

    lax.fori_loop(0, T, finish, 0, unroll=4)


def shards(
    n_row,
    n_col,
    features,
    dw_kernel,
    dw_bias,
    norm_gain,
    norm_bias,
    w_expand,
    b_expand,
    w_reduce,
    b_reduce,
    layer_scale,
    w_query,
    w_keyval,
    rel_bias,
    w_out,
):
    lane = lambda v: v.reshape(1, -1)
    keys = 32 * n_col
    arrays = (
        features, dw_kernel, lane(dw_bias), lane(norm_gain), lane(norm_bias), w_expand,
        lane(b_expand), w_reduce, lane(b_reduce), lane(layer_scale), w_query, w_keyval,
        jnp.transpose(rel_bias, (1, 0, 2)), w_out,
    )
    hbm = pl.BlockSpec(memory_space=pltpu.HBM)
    vmem = pl.BlockSpec(memory_space=pltpu.VMEM)
    return pl.pallas_call(
        functools.partial(kernel, n_row, n_col),
        out_shape=jax.ShapeDtypeStruct(features.shape, BF16),
        in_specs=[hbm] * 14,
        out_specs=vmem,
        scratch_shapes=[pltpu.VMEM(v.shape, v.dtype) for v in arrays]
        + [
            pltpu.VMEM((4, 8, keys), F32),
            pltpu.VMEM((2, (T + 6) * W, 128), F32),
            pltpu.VMEM((2, 10, T + 6, 8, 128), F32),
            pltpu.VMEM((2, 49, 8, 128), F32),
            pltpu.VMEM((2, 128, 8, 128), F32),
            pltpu.VMEM((256, 256), BF16),
            pltpu.VMEM((2, T * T, 128), F32),
            pltpu.VMEM((2, 32, 128), F32),
            pltpu.VMEM((16, 8, keys), F32),
            pltpu.VMEM((2, 3, T, 256), BF16),
            pltpu.VMEM((2, 3, T, 256), BF16),
            pltpu.VMEM((2, 3, T, 256), BF16),
            pltpu.VMEM((4, 3, 16, 256), BF16),
            pltpu.VMEM((n_col, 16, 256), BF16),
            pltpu.SemaphoreType.DMA((14,)),
            pltpu.SemaphoreType.DMA((8,)),
            pltpu.SemaphoreType.DMA((8,)),
            pltpu.SemaphoreType.DMA((n_col - 1,)),
            pltpu.SemaphoreType.DMA((n_col - 1,)),
        ],
        compiler_params=pltpu.CompilerParams(
            collective_id=0, has_side_effects=True, vmem_limit_bytes=40 * 1024 * 1024
        ),
    )(*[pltpu.with_memory_space_constraint(v, pltpu.HBM) for v in arrays])


def solution(mesh):
    return jax.shard_map(
        functools.partial(shards, mesh.shape["row"], mesh.shape["col"]),
        mesh=mesh,
        in_specs=(P("row", "col", None),) + (P(),) * 13,
        out_specs=P("row", "col", None),
        check_vma=False,
    )
```
